256 devices in a mesh: tower: 2 (over core), blk: 16 (over z_lo, x), seq: 8 (over y, z_hi).
Axes of the slice: x: 4, y: 4, z: 8 (z_hi: 2, z_lo: 4; z = z_hi * 4 + z_lo), core: 2. Of those that a mesh axis runs over, the one named last changes fastest.
Arguments:
- queries: bfloat16 [2, 16384, 1024], P('tower', ('blk', 'seq')), may hold values from -6 to 6
- key_rows: bfloat16 [2, 16384, 1024], P('tower', ('blk', 'seq')), may hold values from -6 to 6
- value_rows: bfloat16 [2, 16384, 1024], P('tower', ('blk', 'seq')), may hold values from -6 to 6
- cross_queries: bfloat16 [2, 16384, 1024], P('tower', ('blk', 'seq')), may hold values from -6 to 6
- cross_keys: bfloat16 [2, 16384, 1024], P('tower', ('blk', 'seq')), may hold values from -6 to 6
- cross_values: bfloat16 [2, 16384, 1024], P('tower', ('blk', 'seq')), may hold values from -6 to 6
- grad_out: bfloat16 [2, 16384, 1024], P('tower', ('blk', 'seq')), may hold values from -6 to 6
- offsets: int32 [2, 16], replicated, may hold values from -511 to 511, as said below
- key_valid: int32 [2, 16384], P(None, ('blk', 'seq')), may hold values from 0 to 1, as said below
Outputs:
- attended: bfloat16 [2, 16384, 1024], P('tower', ('blk', 'seq'))
- grad_queries: bfloat16 [2, 16384, 1024], P('tower', ('blk', 'seq'))
- grad_keys: bfloat16 [2, 16384, 1024], P('tower', ('blk', 'seq'))
- grad_values: bfloat16 [2, 16384, 1024], P('tower', ('blk', 'seq'))
- grad_cross_queries: bfloat16 [2, 16384, 1024], P('tower', ('blk', 'seq'))
- grad_cross_keys: bfloat16 [2, 16384, 1024], P('tower', ('blk', 'seq'))
- grad_cross_values: bfloat16 [2, 16384, 1024], P('tower', ('blk', 'seq'))
The draws below stay inside these ranges and needn't reach their ends.
Inputs may be any that keep to these rules, and one draw needn't show every extreme that they name: Both ends of the range occur in every draw; for every block b, offsets[0, b] and offsets[1, b] have opposite signs, and every magnitude is at least 256. `key_valid`: positions k * 1024 + 1024 // 2 - 1 and k * 1024 + 1024 // 2 are always 1.
All inputs are finite; a program needn't handle non-finite values.
Results may differ from the reference program's by a relative error of at most 0.019.
Values may be sent and summed in bfloat16 or wider, within the bound.
No kernel may reach another device: no remote copies, remote signals or barrier semaphores. Data moves between devices by JAX's collectives and lax.ppermute only.
A program may use at most 128 MiB of HBM per device.

```python
import jax
import jax.numpy as jnp
from jax import lax

HEADS = 16
HEAD = 64
D = 1024
LEN = 16384
BLOCK = 1024
NBLOCKS = 16
HALF = 512
QT = 512


def background(key, salt):
    sub_key = jax.random.fold_in(key, salt)
    return jnp.clip(jax.random.normal(sub_key, (2, LEN, HEADS * HEAD), jnp.float32), -4.0, 4.0)


def draw_queries(key, part):
    field = background(key, 1)
    return field.astype(jnp.bfloat16)


def draw_key_rows(key, part):
    field = background(key, 2)
    return field.astype(jnp.bfloat16)


def draw_cross_queries(key, part):
    field = background(key, 3)
    return field.astype(jnp.bfloat16)


def draw_cross_keys(key, part):
    field = background(key, 4)
    return field.astype(jnp.bfloat16)


def draw_offsets(key, part):
    low_mag = max(HALF // 2, 1)
    magnitude = jax.random.randint(key, (2, NBLOCKS), low_mag, HALF)
    sign_first = 2 * jax.random.randint(jax.random.fold_in(key, 7), (NBLOCKS,), 0, 2) - 1
    spots = jax.random.randint(jax.random.fold_in(key, 5), (2,), 0, NBLOCKS)
    sign_first = sign_first.at[spots[0]].set(1).at[spots[1]].set(1)
    magnitude = magnitude.at[0, spots[0]].set(HALF - 1).at[1, spots[1]].set(HALF - 1)
    signs = jnp.stack((sign_first, -sign_first))
    return (signs * magnitude).astype(jnp.int32)


def draw_key_valid(key, part):
    coins = jax.random.randint(key, (2, LEN), 0, 8)
    phase = jnp.arange(LEN) % BLOCK
    keep = (phase == BLOCK // 2 - 1) | (phase == BLOCK // 2)
    return jnp.where(keep[None, :] | (coins > 0), 1, 0).astype(jnp.int32)


def level_of(key, extent, pieces, smallest, high):
    gain, own = 1.0, jax.random.fold_in(key, 6)
    for axis_at, blocks in pieces:
        draws = jnp.exp(jax.random.uniform(jax.random.fold_in(own, axis_at), (blocks,), jnp.float32, smallest / len(pieces), high / len(pieces)))
        gain = gain * jnp.repeat(draws, extent[axis_at] // blocks).reshape([-1 if axis == axis_at else 1 for axis in range(len(extent))])
    return gain


def gaussian(key, extent, width, bound, pieces=(), kind=jnp.bfloat16):
    factor_of = level_of(key, extent, pieces, -0.22, 0.18) if pieces else 1.0
    entries = jax.random.normal(key, extent, jnp.float32) * width * factor_of
    return jnp.minimum(jnp.maximum(entries, -bound), bound).astype(kind)


def setup_inputs(seed: int = 0) -> dict:
    splits = jax.random.split(jax.random.key(seed), 10)
    return {
        "queries": draw_queries(jax.random.fold_in(splits[9], 71), 0),
        "key_rows": draw_key_rows(jax.random.fold_in(splits[9], 71), 0),
        "value_rows": gaussian(splits[2], (2, LEN, D), 1.0, 6.0, ((0, 2), (1, 128))),
        "cross_queries": draw_cross_queries(jax.random.fold_in(splits[9], 71), 0),
        "cross_keys": draw_cross_keys(jax.random.fold_in(splits[9], 71), 0),
        "cross_values": gaussian(splits[5], (2, LEN, D), 1.0, 6.0, ((0, 2), (1, 128))),
        "grad_out": gaussian(splits[6], (2, LEN, D), 1.0, 6.0, ((0, 2), (1, 128))),
        "offsets": draw_offsets(jax.random.fold_in(splits[9], 71), 0),
        "key_valid": draw_key_valid(jax.random.fold_in(splits[9], 71), 0),
    }


def attend(query_tile, grad_tile, key_block, value_block, allowed, heads_here):
    score_scale = HEAD ** -0.5
    rows_count = query_tile.shape[0]
    keys_count = key_block.shape[0]
    q_heads = query_tile.reshape(rows_count, heads_here, HEAD).astype(jnp.float32)
    g_heads = grad_tile.reshape(rows_count, heads_here, HEAD).astype(jnp.float32)
    k_heads = key_block.reshape(keys_count, heads_here, HEAD).astype(jnp.float32)
    v_heads = value_block.reshape(keys_count, heads_here, HEAD).astype(jnp.float32)
    scores = jnp.einsum("qhe,khe->hqk", q_heads, k_heads) * score_scale
    scores = jnp.where(allowed[None], scores, -1e30)
    row_max = jnp.max(scores, axis=2)
    unnormed = jnp.exp(scores - row_max[:, :, None])
    row_sum = jnp.sum(unnormed, axis=2)
    weights = unnormed / row_sum[:, :, None]
    prob_bf = weights.astype(jnp.bfloat16).astype(jnp.float32)
    result = jnp.einsum("hqk,khe->qhe", prob_bf, v_heads).reshape(rows_count, -1)
    grad_probs = jnp.einsum("qhe,khe->hqk", g_heads, v_heads)
    row_dot = jnp.sum(weights * grad_probs, axis=2)
    grad_scores = (weights * (grad_probs - row_dot[:, :, None]) * score_scale).astype(jnp.bfloat16).astype(jnp.float32)
    grad_query = jnp.einsum("hqk,khe->qhe", grad_scores, k_heads).reshape(rows_count, -1)
    grad_key = jnp.einsum("hqk,qhe->khe", grad_scores, q_heads).reshape(keys_count, -1)
    grad_value = jnp.einsum("hqk,qhe->khe", prob_bf, g_heads).reshape(keys_count, -1)
    return result, grad_query, grad_key, grad_value


def reference(queries, key_rows, value_rows, cross_queries, cross_keys, cross_values, grad_out, offsets, key_valid):
    pad_rows = ((HALF, HALF), (0, 0))
    window_span = QT + 2 * HALF
    rows_local = jnp.arange(QT)
    keys_local = jnp.arange(window_span)
    near = jnp.abs(rows_local[:, None] + HALF - keys_local[None, :]) <= HALF
    tiles = jnp.arange(LEN // QT, dtype=jnp.int32)
    zeros_pad = jnp.zeros((LEN + 2 * HALF, HEADS * HEAD), jnp.float32)
    results = []
    cross_key_grads = [None, None]
    cross_value_grads = [None, None]
    for chain in range(2):
        other = 1 - chain
        key_pad = jnp.pad(key_rows[chain], pad_rows)
        value_pad = jnp.pad(value_rows[chain], pad_rows)
        valid_pad = jnp.pad(key_valid[chain], HALF)
        cross_key_pad = jnp.pad(cross_keys[other], pad_rows)
        cross_value_pad = jnp.pad(cross_values[other], pad_rows)
        other_valid = jnp.pad(key_valid[other], HALF)

        def self_step(carry, tile_index):
            grad_key_acc, grad_value_acc = carry
            tile_start = (tile_index * QT).astype(jnp.int32)
            query_tile = lax.dynamic_slice_in_dim(queries[chain], tile_start, QT, 0)
            grad_tile = lax.dynamic_slice_in_dim(grad_out[chain], tile_start, QT, 0)
            key_window = lax.dynamic_slice_in_dim(key_pad, tile_start, window_span, 0)
            value_window = lax.dynamic_slice_in_dim(value_pad, tile_start, window_span, 0)
            allowed = near & (lax.dynamic_slice_in_dim(valid_pad, tile_start, window_span) > 0)[None, :]
            result, grad_query, grad_key, grad_value = attend(query_tile, grad_tile, key_window, value_window, allowed, HEADS)
            grad_key_acc = lax.dynamic_update_slice_in_dim(grad_key_acc, lax.dynamic_slice_in_dim(grad_key_acc, tile_start, window_span, 0) + grad_key, tile_start, 0)
            grad_value_acc = lax.dynamic_update_slice_in_dim(grad_value_acc, lax.dynamic_slice_in_dim(grad_value_acc, tile_start, window_span, 0) + grad_value, tile_start, 0)
            return (grad_key_acc, grad_value_acc), (result, grad_query)

        def cross_step(carry, tile_index):
            grad_key_acc, grad_value_acc = carry
            tile_start = (tile_index * QT).astype(jnp.int32)
            block_index = (tile_start // BLOCK).astype(jnp.int32)
            band_start = (block_index * BLOCK + offsets[chain, block_index] + HALF).astype(jnp.int32)
            query_tile = lax.dynamic_slice_in_dim(cross_queries[chain], tile_start, QT, 0)
            grad_tile = lax.dynamic_slice_in_dim(grad_out[chain], tile_start, QT, 0)
            key_band = lax.dynamic_slice_in_dim(cross_key_pad, band_start, BLOCK, 0)
            value_band = lax.dynamic_slice_in_dim(cross_value_pad, band_start, BLOCK, 0)
            allowed = (lax.dynamic_slice_in_dim(other_valid, band_start, BLOCK) > 0)[None, :]
            result, grad_query, grad_key, grad_value = attend(query_tile, grad_tile, key_band, value_band, allowed, HEADS)
            grad_key_acc = lax.dynamic_update_slice_in_dim(grad_key_acc, lax.dynamic_slice_in_dim(grad_key_acc, band_start, BLOCK, 0) + grad_key, band_start, 0)
            grad_value_acc = lax.dynamic_update_slice_in_dim(grad_value_acc, lax.dynamic_slice_in_dim(grad_value_acc, band_start, BLOCK, 0) + grad_value, band_start, 0)
            return (grad_key_acc, grad_value_acc), (result, grad_query)

        (self_gk, self_gv), (self_out, self_gq) = lax.scan(self_step, (zeros_pad, zeros_pad), tiles)
        (cross_gk, cross_gv), (cross_out, cross_gq) = lax.scan(cross_step, (zeros_pad, zeros_pad), tiles)
        self_out = self_out.reshape(LEN, -1)
        cross_out = cross_out.reshape(LEN, -1)
        attended = (self_out + cross_out).astype(jnp.bfloat16)
        results.append((attended, self_gq.reshape(LEN, -1).astype(jnp.bfloat16), self_gk[HALF:HALF + LEN].astype(jnp.bfloat16), self_gv[HALF:HALF + LEN].astype(jnp.bfloat16), cross_gq.reshape(LEN, -1).astype(jnp.bfloat16)))
        cross_key_grads[other] = cross_gk[HALF:HALF + LEN].astype(jnp.bfloat16)
        cross_value_grads[other] = cross_gv[HALF:HALF + LEN].astype(jnp.bfloat16)
    stacked = [jnp.stack((results[0][slot], results[1][slot])) for slot in range(5)]
    return (stacked[0], stacked[1], stacked[2], stacked[3], stacked[4], jnp.stack(cross_key_grads), jnp.stack(cross_value_grads))
```

```python
import jax
import jax.numpy as jnp
from jax import lax
from jax.experimental import pallas as pl
from jax.experimental.pallas import tpu as pltpu
from jax.sharding import PartitionSpec as P

HEADS = 16
HEAD = 64
BLOCK = 1024
HALF = 512
CHUNK = 128
QROWS = 256
EXT = BLOCK + 2 * HALF
SELF_WIN = QROWS + 2 * HALF
CROSS_WIN = BLOCK + CHUNK
NEG = -16384.0
SCALE = HEAD**-0.5
VROWS = 16
F32 = jnp.float32
BF16 = jnp.bfloat16
NT = (((1,), (1,)), ((), ()))
NN = (((1,), (0,)), ((), ()))


def dot(a, b, dims=NN):
    return lax.dot_general(a, b, dims, preferred_element_type=F32)


def eye(n):
    rows = lax.broadcasted_iota(jnp.int32, (n, n), 0)
    return jnp.where(rows == lax.broadcasted_iota(jnp.int32, (n, n), 1), 1.0, 0.0).astype(BF16)


def flipped(x):
    return dot(eye(x.shape[1]), x, NT).astype(BF16)


def stage_keys(chunks, values, bias, kx, kt, v, vt):
    padded = jnp.concatenate([bias, jnp.zeros((CHUNK - 16, CHUNK), F32)], axis=0).astype(BF16)
    turned = dot(eye(CHUNK), padded, NT)
    lane = lax.broadcasted_iota(jnp.int32, (CHUNK, CHUNK), 1)
    for c in range(EXT // CHUNK):
        at = pl.ds(c * CHUNK, CHUNK)
        k = chunks(c)
        val = values(c)
        kx[at, 0:CHUNK] = k
        kx[at, CHUNK : 2 * CHUNK] = jnp.where(lane == c, turned, 0.0).astype(BF16)
        kt[:, at] = flipped(k)
        v[at, :] = val
        vt[:, at] = flipped(val)


def tile_step(q, gt, start, width, step, windowed, scratch):
    kx, kt, v, vt, s, e, ds, dk, dv = scratch
    count = width // step
    head_lane = lax.broadcasted_iota(jnp.int32, (QROWS, 2 * HEAD), 1) // HEAD
    scaled = q.astype(F32) * SCALE
    ones = jnp.ones((QROWS, CHUNK), BF16)
    win = pl.ds(start, width)
    outs, gqs, q_heads, g_heads = [], [], [], []
    for h in range(2):
        rows_h = slice(h * HEAD, (h + 1) * HEAD)
        cols_h = slice(h * QROWS, (h + 1) * QROWS)
        qh = jnp.where(head_lane == h, scaled, 0.0).astype(BF16)
        qx = jnp.concatenate([qh, ones], axis=1)
        top = None
        for b in range(count):
            at = pl.ds(start + b * step, step)
            scores = dot(kx[at, :], qx, NT)
            if windowed and b in (0, count - 1):
                r = lax.broadcasted_iota(jnp.int32, (step, QROWS), 0)
                c = lax.broadcasted_iota(jnp.int32, (step, QROWS), 1)
                scores = jnp.where(r >= c if b == 0 else r <= c, scores, -1e30)
            s[h, b * step : (b + 1) * step, :] = scores
            high = jnp.max(scores, axis=0, keepdims=True)
            top = high if top is None else jnp.maximum(top, high)
        total = jnp.zeros((1, QROWS), F32)
        for b in range(count):
            rows = slice(b * step, (b + 1) * step)
            p = jnp.exp(s[h, rows, :] - top)
            total = total + jnp.sum(p, axis=0, keepdims=True)
            s[h, rows, :] = p
            e[rows, cols_h] = p.astype(BF16)
        inverse = 1.0 / total
        out = dot(vt[rows_h, win], e[:, cols_h]) * inverse
        g = (gt[rows_h, :].astype(F32) * inverse).astype(BF16)
        row_dot = jnp.sum(out * g.astype(F32), axis=0, keepdims=True)
        zeros = jnp.zeros((HEAD, QROWS), BF16)
        gx = jnp.concatenate([g, zeros] if h == 0 else [zeros, g], axis=0)
        for b in range(count):
            rows = slice(b * step, (b + 1) * step)
            at = pl.ds(start + b * step, step)
            dp = dot(v[at, :], gx)
            ds[rows, cols_h] = (s[h, rows, :] * (dp - row_dot)).astype(BF16)
        gqs.append(dot(kt[rows_h, win], ds[:, cols_h]) * SCALE)
        outs.append(out)
        q_heads.append(qh)
        g_heads.append(gx)
    dv[win, :] += dot(e[...], jnp.concatenate(g_heads, axis=1), NT)
    dk[win, :] += dot(ds[...], jnp.concatenate(q_heads, axis=0))
    return jnp.concatenate(outs, axis=0), jnp.concatenate(gqs, axis=0)


def validity(r1, lo, hi, row):
    parts = [ref[c, 0:VROWS, :].astype(F32)[row : row + 1] for ref, n in ((lo, 4), (r1, 8), (hi, 4)) for c in range(n)]
    return jnp.concatenate(parts, axis=0)


def piece(lo, mid, hi, first):
    def get(c):
        if c < 4:
            return lo[c, first : first + CHUNK, :]
        if c < 12:
            return mid[c - 4, first : first + CHUNK, :]
        return hi[c - 12, first : first + CHUNK, :]

    return get


def emit_sums(dk, dv, pay, at, to_lo, to_hi):
    for n, acc in enumerate((dk, dv)):
        rows = slice(n * CHUNK, (n + 1) * CHUNK)
        spot = slice(at + n * CHUNK, at + (n + 1) * CHUNK)
        to_lo[:, rows, :] = acc[0:HALF, :].astype(BF16).reshape(4, CHUNK, CHUNK)
        pay[:, spot, :] = acc[HALF : HALF + BLOCK, :].astype(BF16).reshape(8, CHUNK, CHUNK)
        to_hi[:, rows, :] = acc[HALF + BLOCK : EXT, :].astype(BF16).reshape(4, CHUNK, CHUNK)


def self_kernel(r1, lo, hi, out_t, pay, to_lo, to_hi, kx, kt, v, vt, gt, s, e, ds, dk, dv):
    bias = jnp.where(validity(r1, lo, hi, 0) > 0.5, 0.0, NEG)
    stage_keys(piece(lo, r1, hi, VROWS), piece(lo, r1, hi, VROWS + CHUNK), bias, kx, kt, v, vt)
    q0, g0 = VROWS + 2 * CHUNK, VROWS + 3 * CHUNK
    for c in range(8):
        gt[:, c * CHUNK : (c + 1) * CHUNK] = flipped(r1[c, g0 : g0 + CHUNK, :])
    dk[...] = jnp.zeros_like(dk)
    dv[...] = jnp.zeros_like(dv)

    def step(i, carry):
        start = pl.multiple_of(i * QROWS, QROWS)
        here = pl.ds(start, QROWS)
        q = r1[pl.ds(2 * i, 2), q0 : q0 + CHUNK, :].reshape(QROWS, CHUNK)
        out, gq = tile_step(q, gt[:, here], start, SELF_WIN, QROWS, True, (kx, kt, v, vt, s, e, ds, dk, dv))
        out_t[:, here] = out
        pay[pl.ds(2 * i, 2), 0:CHUNK, :] = flipped(gq.astype(BF16)).reshape(2, CHUNK, CHUNK)
        return carry

    lax.fori_loop(0, BLOCK // QROWS, step, 0)
    emit_sums(dk, dv, pay, CHUNK, to_lo, to_hi)


def cross_kernel(band, r1, lo, hi, r2, mid, clo, chi, out_t, pay, back, to_lo, to_hi, kx, kt, v, vt, gt, s, e, ds, dk, dv):
    first = band[0]
    place = lax.broadcasted_iota(jnp.int32, (16, CHUNK), 0) * CHUNK + lax.broadcasted_iota(jnp.int32, (16, CHUNK), 1)
    inside = (place >= first) & (place < first + BLOCK)
    bias = jnp.where(inside & (validity(r1, lo, hi, 1) > 0.5), 0.0, NEG)
    stage_keys(piece(clo, mid, chi, 0), piece(clo, mid, chi, CHUNK), bias, kx, kt, v, vt)
    q0, g0 = 2 * CHUNK, VROWS + 3 * CHUNK
    for c in range(8):
        gt[:, c * CHUNK : (c + 1) * CHUNK] = flipped(r1[c, g0 : g0 + CHUNK, :])
    dk[...] = jnp.zeros_like(dk)
    dv[...] = jnp.zeros_like(dv)
    start = pl.multiple_of(lax.shift_right_logical(first, 7) * CHUNK, CHUNK)

    def step(i, carry):
        here = pl.ds(pl.multiple_of(i * QROWS, QROWS), QROWS)
        q = r2[pl.ds(2 * i, 2), q0 : q0 + CHUNK, :].reshape(QROWS, CHUNK)
        out, gq = tile_step(q, gt[:, here], start, CROSS_WIN, 384, False, (kx, kt, v, vt, s, e, ds, dk, dv))
        both = (out + out_t[:, here]).astype(BF16)
        pay[pl.ds(2 * i, 2), 0:CHUNK, :] = flipped(both).reshape(2, CHUNK, CHUNK)
        pay[pl.ds(2 * i, 2), CHUNK : 2 * CHUNK, :] = flipped(gq.astype(BF16)).reshape(2, CHUNK, CHUNK)
        return carry

    lax.fori_loop(0, BLOCK // QROWS, step, 0)
    emit_sums(dk, dv, back, 0, to_lo, to_hi)


def scratch(width):
    return [
        pltpu.VMEM((EXT, 2 * CHUNK), BF16),
        pltpu.VMEM((CHUNK, EXT), BF16),
        pltpu.VMEM((EXT, CHUNK), BF16),
        pltpu.VMEM((CHUNK, EXT), BF16),
        pltpu.VMEM((CHUNK, BLOCK), BF16),
        pltpu.VMEM((2, width, QROWS), F32),
        pltpu.VMEM((width, 2 * QROWS), BF16),
        pltpu.VMEM((width, 2 * QROWS), BF16),
        pltpu.VMEM((EXT, CHUNK), F32),
        pltpu.VMEM((EXT, CHUNK), F32),
    ]


def shaped(shape, dtype=BF16):
    return jax.ShapeDtypeStruct(shape, dtype)


def run_self(r1, lo, hi):
    vmem = pl.BlockSpec(memory_space=pltpu.VMEM)
    return pl.pallas_call(
        self_kernel,
        out_shape=(
            shaped((CHUNK, BLOCK), F32),
            shaped((8, 3 * CHUNK, CHUNK)),
            shaped((4, 2 * CHUNK, CHUNK)),
            shaped((4, 2 * CHUNK, CHUNK)),
        ),
        in_specs=[vmem] * 3,
        out_specs=[vmem] * 4,
        scratch_shapes=scratch(SELF_WIN),
        compiler_params=pltpu.CompilerParams(vmem_limit_bytes=36 * 2**20),
        cost_estimate=pl.CostEstimate(flops=8 * 10**9, bytes_accessed=3 * 2**20, transcendentals=2621440),
        name="self_attention",
    )(r1, lo, hi)


def run_cross(band, r1, lo, hi, r2, mid, clo, chi, out_t):
    vmem = pl.BlockSpec(memory_space=pltpu.VMEM)
    return pl.pallas_call(
        cross_kernel,
        out_shape=(
            shaped((8, 2 * CHUNK, CHUNK)),
            shaped((8, 2 * CHUNK, CHUNK)),
            shaped((4, 2 * CHUNK, CHUNK)),
            shaped((4, 2 * CHUNK, CHUNK)),
        ),
        in_specs=[pl.BlockSpec(memory_space=pltpu.SMEM)] + [vmem] * 8,
        out_specs=[vmem] * 4,
        scratch_shapes=scratch(CROSS_WIN),
        compiler_params=pltpu.CompilerParams(vmem_limit_bytes=36 * 2**20),
        cost_estimate=pl.CostEstimate(flops=8 * 10**9, bytes_accessed=3 * 2**20, transcendentals=2359296),
        name="cross_attention",
    )(band, r1, lo, hi, r2, mid, clo, chi, out_t)


def pieces(rows):
    return rows.reshape(CHUNK, 8, CHUNK).transpose(1, 0, 2)


def exchange(packed):
    return lax.all_to_all(packed, "seq", split_axis=0, concat_axis=0, tiled=True)


def whole(received, n):
    part = received[:, n * CHUNK : (n + 1) * CHUNK, :]
    return part.transpose(1, 0, 2).reshape(1, CHUNK, HEADS * HEAD)


def shards(queries, key_rows, value_rows, cross_queries, cross_keys, cross_values, grad_out, offsets, key_valid):
    tower_id = lax.axis_index("tower")
    block_id = lax.axis_index("blk")
    blocks = lax.axis_size("blk")
    up = [(b, b + 1) for b in range(blocks - 1)]
    down = [(b + 1, b) for b in range(blocks - 1)]
    over_up = [(t * blocks + b, (1 - t) * blocks + b + 1) for t in range(2) for b in range(blocks - 1)]
    over_down = [(t * blocks + b + 1, (1 - t) * blocks + b) for t in range(2) for b in range(blocks - 1)]
    swap = [(0, 1), (1, 0)]
    both = ("tower", "blk")

    own = lax.dynamic_index_in_dim(key_valid, tower_id, 0, keepdims=True)
    other = lax.dynamic_index_in_dim(key_valid, 1 - tower_id, 0, keepdims=True)
    marks = jnp.concatenate([own, other, jnp.zeros((VROWS - 2, CHUNK), jnp.int32)], 0).astype(BF16)
    marks = jnp.broadcast_to(marks[None], (8, VROWS, CHUNK))
    pack1 = jnp.concatenate(
        [marks, pieces(key_rows[0]), pieces(value_rows[0]), pieces(queries[0]), pieces(grad_out[0])], axis=1
    )
    r1 = exchange(pack1)
    pack2 = jnp.concatenate([pieces(cross_keys[0]), pieces(cross_values[0]), pieces(cross_queries[0])], axis=1)
    r2 = exchange(pack2)
    near = VROWS + 2 * CHUNK
    lo = lax.ppermute(r1[4:8, :near], "blk", up)
    hi = lax.ppermute(r1[0:4, :near], "blk", down)
    mid = lax.ppermute(r2[:, : 2 * CHUNK], "tower", swap)
    clo = lax.ppermute(r2[4:8, : 2 * CHUNK], both, over_up)
    chi = lax.ppermute(r2[0:4, : 2 * CHUNK], both, over_down)

    out_t, pay_s, s_lo, s_hi = run_self(r1, lo, hi)
    band = (HALF + offsets[tower_id, block_id]).reshape(1)
    pay_c, back, c_lo, c_hi = run_cross(band, r1, lo, hi, r2, mid, clo, chi, out_t)

    def merged(center, below, above):
        center = center.astype(F32)
        return jnp.concatenate([center[0:4] + below.astype(F32), center[4:8] + above.astype(F32)], 0).astype(BF16)

    above = lax.ppermute(s_lo, "blk", down)
    below = lax.ppermute(s_hi, "blk", up)
    sent_s = jnp.concatenate([pay_s[:, :CHUNK], merged(pay_s[:, CHUNK:], below, above)], axis=1)
    got_s = exchange(sent_s)
    c_above = lax.ppermute(c_lo, both, over_down)
    c_below = lax.ppermute(c_hi, both, over_up)
    c_mid = lax.ppermute(back, "tower", swap)
    sent_c = jnp.concatenate([pay_c, merged(c_mid, c_below, c_above)], axis=1)
    got_c = exchange(sent_c)
    return (
        whole(got_c, 0),
        whole(got_s, 0),
        whole(got_s, 1),
        whole(got_s, 2),
        whole(got_c, 1),
        whole(got_c, 2),
        whole(got_c, 3),
    )


def solution(mesh):
    rows = P("tower", ("blk", "seq"), None)
    in_specs = (rows,) * 7 + (P(), P(None, ("blk", "seq")))
    return jax.shard_map(shards, mesh=mesh, in_specs=in_specs, out_specs=(rows,) * 7, check_vma=False)
```

```python
import functools

import jax
import jax.numpy as jnp
from jax import lax
from jax.experimental import pallas as pl
from jax.experimental.pallas import tpu as pltpu
from jax.sharding import PartitionSpec as P

HEADS = 16
HEAD = 64
BLOCK = 1024
HALF = 512
CHUNK = 128
QROWS = 256
EXT = BLOCK + 2 * HALF
SELF_WIN = QROWS + 2 * HALF
CROSS_WIN = BLOCK + CHUNK
NEG = -16384.0
SCALE = HEAD**-0.5
VROWS = 16
F32 = jnp.float32
BF16 = jnp.bfloat16
NT = (((1,), (1,)), ((), ()))
NN = (((1,), (0,)), ((), ()))


def dot(a, b, dims=NN):
    return lax.dot_general(a, b, dims, preferred_element_type=F32)


def eye(n):
    rows = lax.broadcasted_iota(jnp.int32, (n, n), 0)
    return jnp.where(rows == lax.broadcasted_iota(jnp.int32, (n, n), 1), 1.0, 0.0).astype(BF16)


def flipped(x):
    return dot(eye(x.shape[1]), x, NT).astype(BF16)


def stage_keys(chunks, values, bias, kx, kt, v, vt):
    padded = jnp.concatenate([bias, jnp.zeros((CHUNK - 16, CHUNK), F32)], axis=0).astype(BF16)
    turned = dot(eye(CHUNK), padded, NT)
    lane = lax.broadcasted_iota(jnp.int32, (CHUNK, CHUNK), 1)
    for c in range(EXT // CHUNK):
        at = pl.ds(c * CHUNK, CHUNK)
        k = chunks(c)
        val = values(c)
        kx[at, 0:CHUNK] = k
        kx[at, CHUNK : 2 * CHUNK] = jnp.where(lane == c, turned, 0.0).astype(BF16)
        kt[:, at] = flipped(k)
        v[at, :] = val
        vt[:, at] = flipped(val)


def tile_step(q, gt, start, width, step, windowed, scratch):
    kx, kt, v, vt, s, e, ds, dk, dv = scratch
    count = width // step
    head_lane = lax.broadcasted_iota(jnp.int32, (QROWS, 2 * HEAD), 1) // HEAD
    scaled = q.astype(F32) * SCALE
    ones = jnp.ones((QROWS, CHUNK), BF16)
    win = pl.ds(start, width)
    outs, gqs, q_heads, g_heads, tops, dots = [], [], [], [], [], []
    for h in range(2):
        qh = jnp.where(head_lane == h, scaled, 0.0).astype(BF16)
        qx = jnp.concatenate([qh, ones], axis=1)
        q_heads.append(qh)
        top = None
        for b in range(count):
            at = pl.ds(start + b * step, step)
            scores = dot(kx[at, :], qx, NT)
            if windowed and b in (0, count - 1):
                r = lax.broadcasted_iota(jnp.int32, (step, QROWS), 0)
                c = lax.broadcasted_iota(jnp.int32, (step, QROWS), 1)
                scores = jnp.where(r >= c if b == 0 else r <= c, scores, -1e30)
            s[h, b * step : (b + 1) * step, :] = scores
            high = jnp.max(scores, axis=0, keepdims=True)
            top = high if top is None else jnp.maximum(top, high)
        tops.append(top)
    for h in range(2):
        rows_h = slice(h * HEAD, (h + 1) * HEAD)
        cols_h = slice(h * QROWS, (h + 1) * QROWS)
        total = jnp.zeros((1, QROWS), F32)
        for b in range(count):
            rows = slice(b * step, (b + 1) * step)
            p = jnp.exp(s[h, rows, :] - tops[h])
            total = total + jnp.sum(p, axis=0, keepdims=True)
            e[rows, cols_h] = p.astype(BF16)
        inverse = 1.0 / total
        out = dot(vt[rows_h, win], e[:, cols_h]) * inverse
        g = (gt[rows_h, :].astype(F32) * inverse).astype(BF16)
        dots.append(jnp.sum(out * g.astype(F32), axis=0, keepdims=True))
        zeros = jnp.zeros((HEAD, QROWS), BF16)
        g_heads.append(jnp.concatenate([g, zeros] if h == 0 else [zeros, g], axis=0))
        outs.append(out)
    for h in range(2):
        rows_h = slice(h * HEAD, (h + 1) * HEAD)
        cols_h = slice(h * QROWS, (h + 1) * QROWS)
        for b in range(count):
            rows = slice(b * step, (b + 1) * step)
            at = pl.ds(start + b * step, step)
            dp = dot(v[at, :], g_heads[h])
            ds[rows, cols_h] = (e[rows, cols_h].astype(F32) * (dp - dots[h])).astype(BF16)
        gqs.append(dot(kt[rows_h, win], ds[:, cols_h]) * SCALE)
    dv[win, :] += dot(e[...], jnp.concatenate(g_heads, axis=1), NT)
    dk[win, :] += dot(ds[...], jnp.concatenate(q_heads, axis=0))
    return jnp.concatenate(outs, axis=0), jnp.concatenate(gqs, axis=0)


def validity(refs, row):
    parts = [ref[c, 0:VROWS, :].astype(F32)[row : row + 1] for ref in refs for c in range(4)]
    return jnp.concatenate(parts, axis=0)


def piece(refs, first):
    return lambda c: refs[c // 4][c % 4, first : first + CHUNK, :]


def emit_sums(dk, dv, back, to_lo, to_hi):
    for n, acc in enumerate((dk, dv)):
        rows = slice(n * CHUNK, (n + 1) * CHUNK)
        to_lo[:, rows, :] = acc[0:HALF, :].astype(BF16).reshape(4, CHUNK, CHUNK)
        back[:, rows, :] = acc[HALF : HALF + BLOCK, :].astype(BF16).reshape(8, CHUNK, CHUNK)
        to_hi[:, rows, :] = acc[HALF + BLOCK : EXT, :].astype(BF16).reshape(4, CHUNK, CHUNK)


def self_kernel(before, low, high, after, asks, out_t, pay, back, to_lo, to_hi, kx, kt, v, vt, gt, s, e, ds, dk, dv):
    refs = (before, low, high, after)
    bias = jnp.where(validity(refs, 0) > 0.5, 0.0, NEG)
    stage_keys(piece(refs, VROWS), piece(refs, VROWS + CHUNK), bias, kx, kt, v, vt)
    for c in range(8):
        gt[:, c * CHUNK : (c + 1) * CHUNK] = flipped(asks[c, CHUNK : 2 * CHUNK, :])
    dk[...] = jnp.zeros_like(dk)
    dv[...] = jnp.zeros_like(dv)

    def step(i, carry):
        start = pl.multiple_of(i * QROWS, QROWS)
        here = pl.ds(start, QROWS)
        q = asks[pl.ds(2 * i, 2), 0:CHUNK, :].reshape(QROWS, CHUNK)
        out, gq = tile_step(q, gt[:, here], start, SELF_WIN, QROWS, True, (kx, kt, v, vt, s, e, ds, dk, dv))
        out_t[:, here] = out
        pay[pl.ds(2 * i, 2), 0:CHUNK, :] = flipped(gq.astype(BF16)).reshape(2, CHUNK, CHUNK)
        return carry

    lax.fori_loop(0, BLOCK // QROWS, step, 0)
    emit_sums(dk, dv, back, to_lo, to_hi)


def cross_kernel(pos, before, low, high, after, asks, out_t, pay, back, to_lo, to_hi, kx, kt, v, vt, gt, s, e, ds, dk, dv):
    first = pos[2]
    place = lax.broadcasted_iota(jnp.int32, (16, CHUNK), 0) * CHUNK + lax.broadcasted_iota(jnp.int32, (16, CHUNK), 1)
    inside = (place >= first) & (place < first + BLOCK)
    refs = (before, low, high, after)
    bias = jnp.where(inside & (validity(refs, 1) > 0.5), 0.0, NEG)
    stage_keys(piece(refs, VROWS + 2 * CHUNK), piece(refs, VROWS + 3 * CHUNK), bias, kx, kt, v, vt)
    for c in range(8):
        gt[:, c * CHUNK : (c + 1) * CHUNK] = flipped(asks[c, CHUNK : 2 * CHUNK, :])
    dk[...] = jnp.zeros_like(dk)
    dv[...] = jnp.zeros_like(dv)
    start = pl.multiple_of(lax.shift_right_logical(first, 7) * CHUNK, CHUNK)

    def step(i, carry):
        here = pl.ds(pl.multiple_of(i * QROWS, QROWS), QROWS)
        q = asks[pl.ds(2 * i, 2), 2 * CHUNK : 3 * CHUNK, :].reshape(QROWS, CHUNK)
        out, gq = tile_step(q, gt[:, here], start, CROSS_WIN, 384, False, (kx, kt, v, vt, s, e, ds, dk, dv))
        both = (out + out_t[:, here]).astype(BF16)
        pay[pl.ds(2 * i, 2), 0:CHUNK, :] = flipped(both).reshape(2, CHUNK, CHUNK)
        pay[pl.ds(2 * i, 2), CHUNK : 2 * CHUNK, :] = flipped(gq.astype(BF16)).reshape(2, CHUNK, CHUNK)
        return carry

    lax.fori_loop(0, BLOCK // QROWS, step, 0)
    emit_sums(dk, dv, back, to_lo, to_hi)


def scratch(width):
    return [
        pltpu.VMEM((EXT, 2 * CHUNK), BF16),
        pltpu.VMEM((CHUNK, EXT), BF16),
        pltpu.VMEM((EXT, CHUNK), BF16),
        pltpu.VMEM((CHUNK, EXT), BF16),
        pltpu.VMEM((CHUNK, BLOCK), BF16),
        pltpu.VMEM((2, width, QROWS), F32),
        pltpu.VMEM((width, 2 * QROWS), BF16),
        pltpu.VMEM((width, 2 * QROWS), BF16),
        pltpu.VMEM((EXT, CHUNK), F32),
        pltpu.VMEM((EXT, CHUNK), F32),
    ]


def shaped(shape, dtype=BF16):
    return jax.ShapeDtypeStruct(shape, dtype)


def run_attention(kernel, name, width, operands, outs):
    vmem = pl.BlockSpec(memory_space=pltpu.VMEM)
    outs = outs + (shaped((8, 2 * CHUNK, CHUNK)), shaped((4, 2 * CHUNK, CHUNK)), shaped((4, 2 * CHUNK, CHUNK)))
    return pl.pallas_call(
        kernel,
        out_shape=outs,
        in_specs=[pl.BlockSpec(memory_space=pltpu.SMEM) if x.ndim == 1 else vmem for x in operands],
        out_specs=[vmem] * len(outs),
        scratch_shapes=scratch(width),
        compiler_params=pltpu.CompilerParams(vmem_limit_bytes=14 * 2**20),
        cost_estimate=pl.CostEstimate(flops=8 * 10**9, bytes_accessed=3 * 2**20, transcendentals=2621440),
        name=name,
    )(*operands)


def run_self(*operands):
    outs = (shaped((CHUNK, BLOCK), F32), shaped((8, CHUNK, CHUNK)))
    return run_attention(self_kernel, "self_attention", SELF_WIN, operands, outs)


def run_cross(*operands):
    outs = (shaped((8, 2 * CHUNK, CHUNK)),)
    return run_attention(cross_kernel, "cross_attention", CROSS_WIN, operands, outs)


def small_call(kernel, name, pos, operands, outs):
    vmem = pl.BlockSpec(memory_space=pltpu.VMEM)
    return pl.pallas_call(
        kernel,
        out_shape=outs,
        in_specs=[pl.BlockSpec(memory_space=pltpu.SMEM)] + [vmem] * len(operands),
        out_specs=[vmem] * len(outs),
        compiler_params=pltpu.CompilerParams(vmem_limit_bytes=8 * 2**20),
        cost_estimate=pl.CostEstimate(flops=0, bytes_accessed=2**21, transcendentals=0),
        name=name,
    )(pos, *operands)


def pack_kernel(marked, count, pos, *refs):
    rows, outs = refs[:count], refs[count:]
    at = 0
    if marked:
        valid = rows[0][...].astype(F32)
        own = jnp.where(pos[3] == 0, valid[0:1], valid[1:2])
        other = jnp.where(pos[3] == 0, valid[1:2], valid[0:1])
        marks = jnp.concatenate([own, other, jnp.zeros((VROWS - 2, CHUNK), F32)], axis=0).astype(BF16)
        for out in outs:
            for d in range(4):
                out[d, 0:VROWS, :] = marks
        at, rows = VROWS, rows[1:]
    for n, ref in enumerate(rows):
        spot = slice(at + n * CHUNK, at + (n + 1) * CHUNK)
        for out, z in zip(outs, (pos[1], 1 - pos[1])):
            for d in range(4):
                first = pl.multiple_of((2 * lax.rem(pos[0] + d, 4) + z) * CHUNK, CHUNK)
                out[d, spot, :] = ref[0, :, pl.ds(first, CHUNK)]


def pack(pos, *rows, marked=False):
    height = (len(rows) - 1) * CHUNK + VROWS if marked else len(rows) * CHUNK
    kernel = functools.partial(pack_kernel, marked, len(rows))
    return small_call(kernel, "pack", pos, rows, (shaped((4, height, CHUNK)),) * 2)


def join_kernel(pos, *refs):
    outs = refs[-4:]
    at = 0
    for keep, got in zip(refs[0:-4:2], refs[1:-4:2]):
        rows = slice(at, at + keep.shape[1])
        at += keep.shape[1]
        for d in range(4):
            outs[d][pl.ds(pos[1], 1), rows, :] = keep[d][None]
            outs[d][pl.ds(1 - pos[1], 1), rows, :] = got[d][None]


def join(pos, *pairs):
    height = sum(x.shape[1] for x in pairs[::2])
    return small_call(join_kernel, "join", pos, pairs, (shaped((2, height, CHUNK)),) * 4)


def halves_kernel(pos, *refs):
    parts, (low, high) = refs[:-2], refs[-2:]
    for d in range(4):
        y = lax.rem(pos[0] - d + 4, 4)

        @pl.when(y < 2)
        def _():
            low[pl.ds(2 * y, 2)] = parts[d][...]

        @pl.when(y >= 2)
        def _():
            high[pl.ds(2 * y - 4, 2)] = parts[d][...]


def halves(pos, parts):
    return small_call(halves_kernel, "halves", pos, parts, (shaped((4,) + parts[0].shape[1:]),) * 2)


def whole_kernel(pos, *refs):
    for d in range(4):
        refs[-1][pl.ds(2 * lax.rem(pos[0] - d + 4, 4), 2)] = refs[d][...]


def whole(pos, parts):
    return small_call(whole_kernel, "whole", pos, parts, (shaped((8,) + parts[0].shape[1:]),))[0]


def unpack_kernel(pos, got, *outs):
    for n, out in enumerate(outs):
        for s in range(8):
            out[0, :, s * CHUNK : (s + 1) * CHUNK] = got[s, n * CHUNK : (n + 1) * CHUNK, :]


def unpack(pos, got):
    outs = (shaped((1, CHUNK, HEADS * HEAD)),) * (got.shape[1] // CHUNK)
    return small_call(unpack_kernel, "unpack", pos, (got,), outs)


def merge_kernel(pos, *refs):
    out = refs[-1]
    for n in range(2):
        rows = slice(2 * n * CHUNK, 2 * (n + 1) * CHUNK)
        center, below, above = refs[3 * n : 3 * n + 3]
        for first, halo in ((0, below), (4, above)):
            total = center[first : first + 4].astype(F32) + halo[...].astype(F32)
            out[first : first + 4, rows, :] = total.astype(BF16)


def merge(pos, *parts):
    return small_call(merge_kernel, "merge", pos, parts, (shaped((8, 4 * CHUNK, CHUNK)),))[0]


def order_kernel(pos, *refs):
    outs = refs[-2:]
    at = 0
    for ref in refs[:-2]:
        rows = slice(at, at + ref.shape[1])
        at += ref.shape[1]
        for out, z in zip(outs, (pos[1], 1 - pos[1])):
            for d in range(4):
                out[d, rows, :] = ref[pl.ds(2 * lax.rem(pos[0] + d, 4) + z, 1)][0]


def order(pos, *parts):
    height = sum(x.shape[1] for x in parts)
    return small_call(order_kernel, "order", pos, parts, (shaped((4, height, CHUNK)),) * 2)


def unpack_parts_kernel(pos, *refs):
    parts, outs = refs[:4], refs[4:]
    for d in range(4):
        y = lax.rem(pos[0] - d + 4, 4)
        for n, out in enumerate(outs):
            for z in range(2):
                at = pl.multiple_of((2 * y + z) * CHUNK, CHUNK)
                out[0, :, pl.ds(at, CHUNK)] = parts[d][z, n * CHUNK : (n + 1) * CHUNK, :]


def unpack_parts(pos, parts):
    outs = (shaped((1, CHUNK, HEADS * HEAD)),) * (parts[0].shape[1] // CHUNK)
    return small_call(unpack_parts_kernel, "unpack_parts", pos, parts, outs)


def across_z(send):
    size = lax.axis_size("seq")
    return lax.ppermute(send, "seq", [(i, i ^ 1) for i in range(size)])


def along_y(parts):
    size = lax.axis_size("seq")
    return (parts[0],) + tuple(
        lax.ppermute(parts[d], "seq", [(i, (i + 2 * d) % size) for i in range(size)]) for d in range(1, 4)
    )


def exchange(packed):
    return lax.all_to_all(packed, "seq", split_axis=0, concat_axis=0, tiled=True)


def shards(queries, key_rows, value_rows, cross_queries, cross_keys, cross_values, grad_out, offsets, key_valid):
    tower_id = lax.axis_index("tower")
    block_id = lax.axis_index("blk")
    blocks = lax.axis_size("blk")
    up = [(b, b + 1) for b in range(blocks - 1)]
    down = [(b + 1, b) for b in range(blocks - 1)]
    over_up = [(t * blocks + b, (1 - t) * blocks + b + 1) for t in range(2) for b in range(blocks - 1)]
    over_down = [(t * blocks + b + 1, (1 - t) * blocks + b) for t in range(2) for b in range(blocks - 1)]
    swap = [(0, 1), (1, 0)]
    both = ("tower", "blk")

    seq_id = lax.axis_index("seq")
    band = HALF + offsets[tower_id, block_id]
    pos = jnp.stack([seq_id // 2, seq_id % 2, band, tower_id]).astype(jnp.int32)

    hold = lax.optimization_barrier
    swapped_k = lax.ppermute(cross_keys, "tower", swap)
    swapped_v = lax.ppermute(cross_values, "tower", swap)
    keep_a, send_a = pack(pos, key_valid, key_rows, value_rows, marked=True)
    got_a = across_z(send_a)
    keep_c, send_c = pack(pos, swapped_k, swapped_v)
    queries, send_c = hold((queries, send_c))
    got_c = across_z(send_c)
    keep_b, send_b = pack(pos, queries, grad_out, cross_queries)
    got_b = across_z(send_b)
    low, high = halves(pos, along_y(join(pos, keep_a, got_a, keep_c, got_c)))
    before = lax.ppermute(high, "blk", up)
    after = lax.ppermute(low, "blk", down)
    asks = whole(pos, along_y(join(pos, keep_b, got_b)))

    out_t, pay_q, center, to_lo, to_hi = run_self(before, low, high, after, asks)
    above = lax.ppermute(to_lo, "blk", down)
    below = lax.ppermute(to_hi, "blk", up)
    pay_x, back, c_lo, c_hi = run_cross(pos, before, low, high, after, asks, out_t)
    keep_p, send_p = order(pos, pay_q, pay_x)
    got_p = across_z(send_p)
    c_above = lax.ppermute(c_lo, both, over_down)
    c_below = lax.ppermute(c_hi, both, over_up)
    c_mid = lax.ppermute(back, "tower", swap)
    got_p, center = hold((got_p, center))
    got_s = exchange(merge(pos, center, below, above, c_mid, c_below, c_above))
    g_q, attended, g_cq = unpack_parts(pos, along_y(join(pos, keep_p, got_p)))
    g_k, g_v, g_ck, g_cv = unpack(pos, got_s)
    return attended, g_q, g_k, g_v, g_cq, g_ck, g_cv


def solution(mesh):
    rows = P("tower", ("blk", "seq"), None)
    in_specs = (rows,) * 7 + (P(), P(None, ("blk", "seq")))
    return jax.shard_map(shards, mesh=mesh, in_specs=in_specs, out_specs=(rows,) * 7, check_vma=False)
```

```python
import functools

import jax
import jax.numpy as jnp
from jax import lax
from jax.experimental import pallas as pl
from jax.experimental.pallas import tpu as pltpu
from jax.sharding import PartitionSpec as P

HEADS = 16
HEAD = 64
BLOCK = 1024
HALF = 512
CHUNK = 128
QROWS = 256
EXT = BLOCK + 2 * HALF
SELF_WIN = QROWS + 2 * HALF
CROSS_WIN = BLOCK + CHUNK
NEG = -16384.0
SCALE = HEAD**-0.5
VROWS = 16
F32 = jnp.float32
BF16 = jnp.bfloat16
NT = (((1,), (1,)), ((), ()))
NN = (((1,), (0,)), ((), ()))


def dot(a, b, dims=NN):
    return lax.dot_general(a, b, dims, preferred_element_type=F32)


def eye(n):
    rows = lax.broadcasted_iota(jnp.int32, (n, n), 0)
    return jnp.where(rows == lax.broadcasted_iota(jnp.int32, (n, n), 1), 1.0, 0.0).astype(BF16)


def flipped(x):
    return dot(eye(x.shape[1]), x, NT).astype(BF16)


def stage_keys(chunks, values, bias, kx, kt, v, vt):
    padded = jnp.concatenate([bias, jnp.zeros((CHUNK - 16, CHUNK), F32)], axis=0).astype(BF16)
    turned = dot(eye(CHUNK), padded, NT)
    lane = lax.broadcasted_iota(jnp.int32, (CHUNK, CHUNK), 1)
    for c in range(EXT // CHUNK):
        at = pl.ds(c * CHUNK, CHUNK)
        k = chunks(c)
        val = values(c)
        kx[at, 0:CHUNK] = k
        kx[at, CHUNK : 2 * CHUNK] = jnp.where(lane == c, turned, 0.0).astype(BF16)
        kt[:, at] = flipped(k)
        v[at, :] = val
        vt[:, at] = flipped(val)


def tile_step(q, gt, start, width, step, windowed, scratch):
    kx, kt, v, vt, s, e, ds, dk, dv = scratch
    count = width // step
    head_lane = lax.broadcasted_iota(jnp.int32, (QROWS, 2 * HEAD), 1) // HEAD
    scaled = q.astype(F32) * SCALE
    ones = jnp.ones((QROWS, CHUNK), BF16)
    win = pl.ds(start, width)
    outs, gqs, q_heads, g_heads, tops, dots = [], [], [], [], [], []
    for h in range(2):
        qh = jnp.where(head_lane == h, scaled, 0.0).astype(BF16)
        qx = jnp.concatenate([qh, ones], axis=1)
        q_heads.append(qh)
        top = None
        for b in range(count):
            at = pl.ds(start + b * step, step)
            scores = dot(kx[at, :], qx, NT)
            if windowed and b in (0, count - 1):
                r = lax.broadcasted_iota(jnp.int32, (step, QROWS), 0)
                c = lax.broadcasted_iota(jnp.int32, (step, QROWS), 1)
                scores = jnp.where(r >= c if b == 0 else r <= c, scores, -1e30)
            s[h, b * step : (b + 1) * step, :] = scores
            high = jnp.max(scores, axis=0, keepdims=True)
            top = high if top is None else jnp.maximum(top, high)
        tops.append(top)
    for h in range(2):
        rows_h = slice(h * HEAD, (h + 1) * HEAD)
        cols_h = slice(h * QROWS, (h + 1) * QROWS)
        total = jnp.zeros((1, QROWS), F32)
        for b in range(count):
            rows = slice(b * step, (b + 1) * step)
            p = jnp.exp(s[h, rows, :] - tops[h])
            total = total + jnp.sum(p, axis=0, keepdims=True)
            e[rows, cols_h] = p.astype(BF16)
        inverse = 1.0 / total
        out = dot(vt[rows_h, win], e[:, cols_h]) * inverse
        g = (gt[rows_h, :].astype(F32) * inverse).astype(BF16)
        dots.append(jnp.sum(out * g.astype(F32), axis=0, keepdims=True))
        zeros = jnp.zeros((HEAD, QROWS), BF16)
        g_heads.append(jnp.concatenate([g, zeros] if h == 0 else [zeros, g], axis=0))
        outs.append(out)
    for h in range(2):
        rows_h = slice(h * HEAD, (h + 1) * HEAD)
        cols_h = slice(h * QROWS, (h + 1) * QROWS)
        for b in range(count):
            rows = slice(b * step, (b + 1) * step)
            at = pl.ds(start + b * step, step)
            dp = dot(v[at, :], g_heads[h])
            ds[rows, cols_h] = (e[rows, cols_h].astype(F32) * (dp - dots[h])).astype(BF16)
        gqs.append(dot(kt[rows_h, win], ds[:, cols_h]) * SCALE)
    dv[win, :] += dot(e[...], jnp.concatenate(g_heads, axis=1), NT)
    dk[win, :] += dot(ds[...], jnp.concatenate(q_heads, axis=0))
    return jnp.concatenate(outs, axis=0), jnp.concatenate(gqs, axis=0)


def validity(refs, row):
    parts = [ref[c, 0:VROWS, :].astype(F32)[row : row + 1] for ref in refs for c in range(4)]
    return jnp.concatenate(parts, axis=0)


def piece(refs, first):
    return lambda c: refs[c // 4][c % 4, first : first + CHUNK, :]


def emit_sums(dk, dv, back, to_lo, to_hi):
    for n, acc in enumerate((dk, dv)):
        rows = slice(n * CHUNK, (n + 1) * CHUNK)
        to_lo[:, rows, :] = acc[0:HALF, :].astype(BF16).reshape(4, CHUNK, CHUNK)
        back[:, rows, :] = acc[HALF : HALF + BLOCK, :].astype(BF16).reshape(8, CHUNK, CHUNK)
        to_hi[:, rows, :] = acc[HALF + BLOCK : EXT, :].astype(BF16).reshape(4, CHUNK, CHUNK)


def self_kernel(before, low, high, after, asks, out_t, gt, pay, back, to_lo, to_hi, kx, kt, v, vt, s, e, ds, dk, dv):
    refs = (before, low, high, after)
    bias = jnp.where(validity(refs, 0) > 0.5, 0.0, NEG)
    stage_keys(piece(refs, VROWS), piece(refs, VROWS + CHUNK), bias, kx, kt, v, vt)
    for c in range(8):
        gt[:, c * CHUNK : (c + 1) * CHUNK] = flipped(asks[c, CHUNK : 2 * CHUNK, :])
    dk[...] = jnp.zeros_like(dk)
    dv[...] = jnp.zeros_like(dv)

    def step(i, carry):
        start = pl.multiple_of(i * QROWS, QROWS)
        here = pl.ds(start, QROWS)
        q = asks[pl.ds(2 * i, 2), 0:CHUNK, :].reshape(QROWS, CHUNK)
        out, gq = tile_step(q, gt[:, here], start, SELF_WIN, QROWS, True, (kx, kt, v, vt, s, e, ds, dk, dv))
        out_t[:, here] = out
        pay[pl.ds(2 * i, 2), 0:CHUNK, :] = flipped(gq.astype(BF16)).reshape(2, CHUNK, CHUNK)
        return carry

    lax.fori_loop(0, BLOCK // QROWS, step, 0)
    emit_sums(dk, dv, back, to_lo, to_hi)


def cross_kernel(band, vb, vl, vh, va, before, low, high, after, asks, out_t, gt, pay, back, to_lo, to_hi, kx, kt, v, vt, s, e, ds, dk, dv):
    first = band[0]
    place = lax.broadcasted_iota(jnp.int32, (16, CHUNK), 0) * CHUNK + lax.broadcasted_iota(jnp.int32, (16, CHUNK), 1)
    inside = (place >= first) & (place < first + BLOCK)
    refs = (before, low, high, after)
    bias = jnp.where(inside & (validity((vb, vl, vh, va), 1) > 0.5), 0.0, NEG)
    stage_keys(piece(refs, 0), piece(refs, CHUNK), bias, kx, kt, v, vt)
    dk[...] = jnp.zeros_like(dk)
    dv[...] = jnp.zeros_like(dv)
    start = pl.multiple_of(lax.shift_right_logical(first, 7) * CHUNK, CHUNK)

    def step(i, carry):
        here = pl.ds(pl.multiple_of(i * QROWS, QROWS), QROWS)
        q = asks[pl.ds(2 * i, 2), 2 * CHUNK : 3 * CHUNK, :].reshape(QROWS, CHUNK)
        out, gq = tile_step(q, gt[:, here], start, CROSS_WIN, 384, False, (kx, kt, v, vt, s, e, ds, dk, dv))
        both = (out + out_t[:, here]).astype(BF16)
        pay[pl.ds(2 * i, 2), 0:CHUNK, :] = flipped(both).reshape(2, CHUNK, CHUNK)
        pay[pl.ds(2 * i, 2), CHUNK : 2 * CHUNK, :] = flipped(gq.astype(BF16)).reshape(2, CHUNK, CHUNK)
        return carry

    lax.fori_loop(0, BLOCK // QROWS, step, 0)
    emit_sums(dk, dv, back, to_lo, to_hi)


def scratch(width):
    return [
        pltpu.VMEM((EXT, 2 * CHUNK), BF16),
        pltpu.VMEM((CHUNK, EXT), BF16),
        pltpu.VMEM((EXT, CHUNK), BF16),
        pltpu.VMEM((CHUNK, EXT), BF16),
        pltpu.VMEM((2, width, QROWS), F32),
        pltpu.VMEM((width, 2 * QROWS), BF16),
        pltpu.VMEM((width, 2 * QROWS), BF16),
        pltpu.VMEM((EXT, CHUNK), F32),
        pltpu.VMEM((EXT, CHUNK), F32),
    ]


def shaped(shape, dtype=BF16):
    return jax.ShapeDtypeStruct(shape, dtype)


def run_attention(kernel, name, width, operands, outs):
    vmem = pl.BlockSpec(memory_space=pltpu.VMEM)
    outs = outs + (shaped((8, 2 * CHUNK, CHUNK)), shaped((4, 2 * CHUNK, CHUNK)), shaped((4, 2 * CHUNK, CHUNK)))
    return pl.pallas_call(
        kernel,
        out_shape=outs,
        in_specs=[pl.BlockSpec(memory_space=pltpu.SMEM) if x.ndim == 1 else vmem for x in operands],
        out_specs=[vmem] * len(outs),
        scratch_shapes=scratch(width),
        compiler_params=pltpu.CompilerParams(vmem_limit_bytes=14 * 2**20),
        cost_estimate=pl.CostEstimate(flops=8 * 10**9, bytes_accessed=3 * 2**20, transcendentals=2621440),
        name=name,
    )(*operands)


def run_self(*operands):
    outs = (shaped((CHUNK, BLOCK), F32), shaped((CHUNK, BLOCK)), shaped((8, CHUNK, CHUNK)))
    return run_attention(self_kernel, "self_attention", SELF_WIN, operands, outs)


def run_cross(*operands):
    outs = (shaped((8, 2 * CHUNK, CHUNK)),)
    return run_attention(cross_kernel, "cross_attention", CROSS_WIN, operands, outs)


def small_call(kernel, name, pos, operands, outs):
    vmem = pl.BlockSpec(memory_space=pltpu.VMEM)
    return pl.pallas_call(
        kernel,
        out_shape=outs,
        in_specs=[pl.BlockSpec(memory_space=pltpu.SMEM)] + [vmem] * len(operands),
        out_specs=[vmem] * len(outs),
        compiler_params=pltpu.CompilerParams(vmem_limit_bytes=8 * 2**20),
        cost_estimate=pl.CostEstimate(flops=0, bytes_accessed=2**21, transcendentals=0),
        name=name,
    )(pos, *operands)


def column_pieces(pos, ref, keep, send, spot):
    for out, z in ((keep, pos[1]), (send, 1 - pos[1])):
        for d in range(4):
            first = pl.multiple_of((2 * lax.rem(pos[0] + d, 4) + z) * CHUNK, CHUNK)
            out[d, spot, :] = ref[0, :, pl.ds(first, CHUNK)]


def pack_kernel(pos, *refs):
    for n, ref in enumerate(refs[:-2]):
        column_pieces(pos, ref, *refs[-2:], slice(n * CHUNK, (n + 1) * CHUNK))


def pack(pos, *rows):
    return small_call(pack_kernel, "pack", pos, rows, (shaped((4, len(rows) * CHUNK, CHUNK)),) * 2)


def pack_marked_kernel(pos, key_valid, keys, values, keep, send, held_k, held_v, sems):
    copies = [pltpu.make_async_copy(keys, held_k, sems.at[0]), pltpu.make_async_copy(values, held_v, sems.at[1])]
    for copy in copies:
        copy.start()
    valid = key_valid[...].astype(F32)
    own = jnp.where(pos[2] == 0, valid[0:1], valid[1:2])
    other = jnp.where(pos[2] == 0, valid[1:2], valid[0:1])
    marks = jnp.concatenate([own, other, jnp.zeros((VROWS - 2, CHUNK), F32)], axis=0).astype(BF16)
    for out in (keep, send):
        for d in range(4):
            out[d, 0:VROWS, :] = marks
    for n, (copy, held) in enumerate(zip(copies, (held_k, held_v))):
        copy.wait()
        column_pieces(pos, held, keep, send, slice(VROWS + n * CHUNK, VROWS + (n + 1) * CHUNK))


def pack_marked(pos, key_valid, keys, values):
    vmem = pl.BlockSpec(memory_space=pltpu.VMEM)
    whole_hbm = pl.BlockSpec(memory_space=pl.ANY)
    return pl.pallas_call(
        pack_marked_kernel,
        out_shape=(shaped((4, VROWS + 2 * CHUNK, CHUNK)),) * 2,
        in_specs=[pl.BlockSpec(memory_space=pltpu.SMEM), vmem, whole_hbm, whole_hbm],
        out_specs=[vmem] * 2,
        scratch_shapes=[pltpu.VMEM(keys.shape, BF16), pltpu.VMEM(values.shape, BF16), pltpu.SemaphoreType.DMA((2,))],
        cost_estimate=pl.CostEstimate(flops=0, bytes_accessed=2**21, transcendentals=0),
        name="pack_marked",
    )(pos, key_valid, keys, values)


def join_kernel(pos, *refs):
    outs = refs[-4:]
    at = 0
    for keep, got in zip(refs[0:-4:2], refs[1:-4:2]):
        rows = slice(at, at + keep.shape[1])
        at += keep.shape[1]
        for d in range(4):
            outs[d][pl.ds(pos[1], 1), rows, :] = keep[d][None]
            outs[d][pl.ds(1 - pos[1], 1), rows, :] = got[d][None]


def join(pos, *pairs):
    height = sum(x.shape[1] for x in pairs[::2])
    return small_call(join_kernel, "join", pos, pairs, (shaped((2, height, CHUNK)),) * 4)


def halves_kernel(pos, *refs):
    parts, (low, high) = refs[:-2], refs[-2:]
    for d in range(4):
        y = lax.rem(pos[0] - d + 4, 4)

        @pl.when(y < 2)
        def _():
            low[pl.ds(2 * y, 2)] = parts[d][...]

        @pl.when(y >= 2)
        def _():
            high[pl.ds(2 * y - 4, 2)] = parts[d][...]


def halves(pos, parts):
    return small_call(halves_kernel, "halves", pos, parts, (shaped((4,) + parts[0].shape[1:]),) * 2)


def pack_y_kernel(pos, *refs):
    rows, outs = refs[:-4], refs[-4:]
    for n, ref in enumerate(rows):
        for d in range(4):
            first = pl.multiple_of(2 * lax.rem(pos[0] + d, 4) * CHUNK, 2 * CHUNK)
            pair = ref[0, :, pl.ds(first, 2 * CHUNK)]
            outs[d][0, n * CHUNK : (n + 1) * CHUNK, :] = pair[:, 0:CHUNK]
            outs[d][1, n * CHUNK : (n + 1) * CHUNK, :] = pair[:, CHUNK:]


def pack_y(pos, *rows):
    return small_call(pack_y_kernel, "pack_y", pos, rows, (shaped((2, len(rows) * CHUNK, CHUNK)),) * 4)


def split_kernel(pos, *refs):
    keep, send = refs[4:]
    for d in range(4):
        keep[d] = refs[d][pl.ds(pos[1], 1)][0]
        send[d] = refs[d][pl.ds(1 - pos[1], 1)][0]


def split(pos, parts):
    return small_call(split_kernel, "split", pos, parts, (shaped((4,) + parts[0].shape[1:]),) * 2)


def whole_kernel(pos, keep, got, out):
    for d in range(4):
        at = 2 * lax.rem(pos[0] - d + 4, 4)
        out[pl.ds(at + pos[1], 1)] = keep[d][None]
        out[pl.ds(at + 1 - pos[1], 1)] = got[d][None]


def whole(pos, keep, got):
    return small_call(whole_kernel, "whole", pos, (keep, got), (shaped((8,) + keep.shape[1:]),))[0]


def unpack_kernel(pos, got, *outs):
    for n, out in enumerate(outs):
        for s in range(8):
            out[0, :, s * CHUNK : (s + 1) * CHUNK] = got[s, n * CHUNK : (n + 1) * CHUNK, :]


def unpack(pos, got):
    outs = (shaped((1, CHUNK, HEADS * HEAD)),) * (got.shape[1] // CHUNK)
    return small_call(unpack_kernel, "unpack", pos, (got,), outs)


def merge_kernel(pos, *refs):
    out = refs[-1]
    for n in range(2):
        rows = slice(2 * n * CHUNK, 2 * (n + 1) * CHUNK)
        center, below, above = refs[3 * n : 3 * n + 3]
        for first, halo in ((0, below), (4, above)):
            total = center[first : first + 4].astype(F32) + halo[...].astype(F32)
            out[first : first + 4, rows, :] = total.astype(BF16)


def merge(pos, *parts):
    return small_call(merge_kernel, "merge", pos, parts, (shaped((8, 4 * CHUNK, CHUNK)),))[0]


def order_kernel(pos, *refs):
    outs = refs[-2:]
    at = 0
    for ref in refs[:-2]:
        rows = slice(at, at + ref.shape[1])
        at += ref.shape[1]
        for out, z in zip(outs, (pos[1], 1 - pos[1])):
            for d in range(4):
                out[d, rows, :] = ref[pl.ds(2 * lax.rem(pos[0] + d, 4) + z, 1)][0]


def order(pos, *parts):
    height = sum(x.shape[1] for x in parts)
    return small_call(order_kernel, "order", pos, parts, (shaped((4, height, CHUNK)),) * 2)


def unpack_parts_kernel(pos, *refs):
    parts, outs = refs[:4], refs[4:]
    for d in range(4):
        y = lax.rem(pos[0] - d + 4, 4)
        for n, out in enumerate(outs):
            for z in range(2):
                at = pl.multiple_of((2 * y + z) * CHUNK, CHUNK)
                out[0, :, pl.ds(at, CHUNK)] = parts[d][z, n * CHUNK : (n + 1) * CHUNK, :]


def unpack_parts(pos, parts):
    outs = (shaped((1, CHUNK, HEADS * HEAD)),) * (parts[0].shape[1] // CHUNK)
    return small_call(unpack_parts_kernel, "unpack_parts", pos, parts, outs)


def across_z(send):
    size = lax.axis_size("seq")
    return lax.ppermute(send, "seq", [(i, i ^ 1) for i in range(size)])


def along_y(parts):
    size = lax.axis_size("seq")
    return (parts[0],) + tuple(
        lax.ppermute(parts[d], "seq", [(i, (i + 2 * d) % size) for i in range(size)]) for d in range(1, 4)
    )


def exchange(packed):
    return lax.all_to_all(packed, "seq", split_axis=0, concat_axis=0, tiled=True)


def shards(queries, key_rows, value_rows, cross_queries, cross_keys, cross_values, grad_out, offsets, key_valid):
    tower_id = lax.axis_index("tower")
    block_id = lax.axis_index("blk")
    blocks = lax.axis_size("blk")
    up = [(b, b + 1) for b in range(blocks - 1)]
    down = [(b + 1, b) for b in range(blocks - 1)]
    over_up = [(t * blocks + b, (1 - t) * blocks + b + 1) for t in range(2) for b in range(blocks - 1)]
    over_down = [(t * blocks + b + 1, (1 - t) * blocks + b) for t in range(2) for b in range(blocks - 1)]
    swap = [(0, 1), (1, 0)]
    both = ("tower", "blk")

    seq_id = lax.axis_index("seq")
    pos = jnp.stack([seq_id // 2, seq_id % 2, tower_id]).astype(jnp.int32)
    band = (HALF + offsets[tower_id, block_id]).reshape(1)
    hold = lax.optimization_barrier
    swapped_k = lax.ppermute(cross_keys, "tower", swap)
    swapped_v = lax.ppermute(cross_values, "tower", swap)
    keep_a, send_a = pack_marked(pos, key_valid, key_rows, value_rows)
    got_a = across_z(send_a)
    keep_c, send_c = pack(pos, swapped_k, swapped_v)
    got_c = across_z(send_c)
    keep_b, send_b = split(pos, along_y(pack_y(pos, queries, grad_out, cross_queries)))
    got_b = across_z(send_b)
    low, high = halves(pos, along_y(join(pos, keep_a, got_a)))
    before = lax.ppermute(high, "blk", up)
    after = lax.ppermute(low, "blk", down)
    c_low, c_high = halves(pos, along_y(join(pos, keep_c, got_c)))
    got_b, c_low, c_high = hold((got_b, c_low, c_high))
    c_before = lax.ppermute(c_high, "blk", up)
    c_after = lax.ppermute(c_low, "blk", down)
    asks = whole(pos, keep_b, got_b)

    out_t, turned, pay_q, center, to_lo, to_hi = run_self(before, low, high, after, asks)
    above = lax.ppermute(to_lo, "blk", down)
    below = lax.ppermute(to_hi, "blk", up)
    pay_x, back, c_lo, c_hi = run_cross(
        band, before, low, high, after, c_before, c_low, c_high, c_after, asks, out_t, turned
    )
    keep_p, send_p = order(pos, pay_q, pay_x)
    got_p = across_z(send_p)
    c_above = lax.ppermute(c_lo, both, over_down)
    c_below = lax.ppermute(c_hi, both, over_up)
    c_mid = lax.ppermute(back, "tower", swap)
    got_p, center = hold((got_p, center))
    got_s = exchange(merge(pos, center, below, above, c_mid, c_below, c_above))
    g_q, attended, g_cq = unpack_parts(pos, along_y(join(pos, keep_p, got_p)))
    g_k, g_v, g_ck, g_cv = unpack(pos, got_s)
    return attended, g_q, g_k, g_v, g_cq, g_ck, g_cv


def solution(mesh):
    rows = P("tower", ("blk", "seq"), None)
    in_specs = (rows,) * 7 + (P(), P(None, ("blk", "seq")))
    return jax.shard_map(shards, mesh=mesh, in_specs=in_specs, out_specs=(rows,) * 7, check_vma=False)
```

```python
import functools

import jax
import jax.numpy as jnp
from jax import lax
from jax.experimental import pallas as pl
from jax.experimental.pallas import tpu as pltpu
from jax.sharding import PartitionSpec as P

HEADS = 16
HEAD = 64
BLOCK = 1024
HALF = 512
CHUNK = 128
QROWS = 256
EXT = BLOCK + 2 * HALF
SELF_WIN = QROWS + 2 * HALF
CROSS_WIN = BLOCK + CHUNK
NEG = -16384.0
SCALE = HEAD**-0.5
VROWS = 16
F32 = jnp.float32
BF16 = jnp.bfloat16
NT = (((1,), (1,)), ((), ()))
NN = (((1,), (0,)), ((), ()))


def dot(a, b, dims=NN):
    return lax.dot_general(a, b, dims, preferred_element_type=F32)


def eye(n):
    rows = lax.broadcasted_iota(jnp.int32, (n, n), 0)
    return jnp.where(rows == lax.broadcasted_iota(jnp.int32, (n, n), 1), 1.0, 0.0).astype(BF16)


def flipped(x):
    return dot(eye(x.shape[1]), x, NT).astype(BF16)


def stage_keys(chunks, values, bias, kx, kt, v, vt):
    padded = jnp.concatenate([bias, jnp.zeros((CHUNK - 16, CHUNK), F32)], axis=0).astype(BF16)
    turned = dot(eye(CHUNK), padded, NT)
    lane = lax.broadcasted_iota(jnp.int32, (CHUNK, CHUNK), 1)
    for c in range(0, EXT // CHUNK, 2):
        pair = pl.ds(c * CHUNK, 2 * CHUNK)
        k = jnp.concatenate([chunks(c), chunks(c + 1)], axis=0)
        val = jnp.concatenate([values(c), values(c + 1)], axis=0)
        kx[pair, 0:CHUNK] = k
        for n in range(2):
            kx[pl.ds((c + n) * CHUNK, CHUNK), CHUNK : 2 * CHUNK] = jnp.where(lane == c + n, turned, 0.0).astype(BF16)
        kt[:, pair] = flipped(k)
        v[pair, :] = val
        vt[:, pair] = flipped(val)


def tile_step(q, gt, start, width, step, windowed, scratch):
    kx, kt, v, vt, s, e, ds, dk, dv = scratch
    count = width // step
    head_lane = lax.broadcasted_iota(jnp.int32, (QROWS, 2 * HEAD), 1) // HEAD
    scaled = q.astype(F32) * SCALE
    ones = jnp.ones((QROWS, CHUNK), BF16)
    win = pl.ds(start, width)
    outs, gqs, q_heads, g_heads, tops, dots = [], [], [], [], [], []
    for h in range(2):
        qh = jnp.where(head_lane == h, scaled, 0.0).astype(BF16)
        qx = jnp.concatenate([qh, ones], axis=1)
        q_heads.append(qh)
        top = None
        for b in range(count):
            at = pl.ds(start + b * step, step)
            scores = dot(kx[at, :], qx, NT)
            if windowed and b in (0, count - 1):
                r = lax.broadcasted_iota(jnp.int32, (step, QROWS), 0)
                c = lax.broadcasted_iota(jnp.int32, (step, QROWS), 1)
                scores = jnp.where(r >= c if b == 0 else r <= c, scores, -1e30)
            s[h, b * step : (b + 1) * step, :] = scores
            high = jnp.max(scores, axis=0, keepdims=True)
            top = high if top is None else jnp.maximum(top, high)
        tops.append(top)
    for h in range(2):
        rows_h = slice(h * HEAD, (h + 1) * HEAD)
        cols_h = slice(h * QROWS, (h + 1) * QROWS)
        total = jnp.zeros((1, QROWS), F32)
        for b in range(count):
            rows = slice(b * step, (b + 1) * step)
            p = jnp.exp(s[h, rows, :] - tops[h])
            total = total + jnp.sum(p, axis=0, keepdims=True)
            e[rows, cols_h] = p.astype(BF16)
        inverse = 1.0 / total
        out = dot(vt[rows_h, win], e[:, cols_h]) * inverse
        g = (gt[rows_h, :].astype(F32) * inverse).astype(BF16)
        dots.append(jnp.sum(out * g.astype(F32), axis=0, keepdims=True))
        zeros = jnp.zeros((HEAD, QROWS), BF16)
        g_heads.append(jnp.concatenate([g, zeros] if h == 0 else [zeros, g], axis=0))
        outs.append(out)
    for h in range(2):
        rows_h = slice(h * HEAD, (h + 1) * HEAD)
        cols_h = slice(h * QROWS, (h + 1) * QROWS)
        for b in range(count):
            rows = slice(b * step, (b + 1) * step)
            at = pl.ds(start + b * step, step)
            dp = dot(v[at, :], g_heads[h])
            ds[rows, cols_h] = (e[rows, cols_h].astype(F32) * (dp - dots[h])).astype(BF16)
        gqs.append(dot(kt[rows_h, win], ds[:, cols_h]) * SCALE)
    dv[win, :] += dot(e[...], jnp.concatenate(g_heads, axis=1), NT)
    dk[win, :] += dot(ds[...], jnp.concatenate(q_heads, axis=0))
    return jnp.concatenate(outs, axis=0), jnp.concatenate(gqs, axis=0)


def validity(refs, row):
    parts = [ref[c, 0:VROWS, :].astype(F32)[row : row + 1] for ref in refs for c in range(4)]
    return jnp.concatenate(parts, axis=0)


def piece(refs, first):
    return lambda c: refs[c // 4][c % 4, first : first + CHUNK, :]


def emit_sums(dk, dv, back, to_lo, to_hi):
    for n, acc in enumerate((dk, dv)):
        rows = slice(n * CHUNK, (n + 1) * CHUNK)
        to_lo[:, rows, :] = acc[0:HALF, :].astype(BF16).reshape(4, CHUNK, CHUNK)
        back[:, rows, :] = acc[HALF : HALF + BLOCK, :].astype(BF16).reshape(8, CHUNK, CHUNK)
        to_hi[:, rows, :] = acc[HALF + BLOCK : EXT, :].astype(BF16).reshape(4, CHUNK, CHUNK)


def self_kernel(before, low, high, after, asks, out_t, gt, pay, back, to_lo, to_hi, kx, kt, v, vt, s, e, ds, dk, dv):
    refs = (before, low, high, after)
    bias = jnp.where(validity(refs, 0) > 0.5, 0.0, NEG)
    stage_keys(piece(refs, VROWS), piece(refs, VROWS + CHUNK), bias, kx, kt, v, vt)
    for c in range(0, 8, 2):
        pair = jnp.concatenate([asks[c, CHUNK : 2 * CHUNK, :], asks[c + 1, CHUNK : 2 * CHUNK, :]], axis=0)
        gt[:, c * CHUNK : (c + 2) * CHUNK] = flipped(pair)
    dk[...] = jnp.zeros_like(dk)
    dv[...] = jnp.zeros_like(dv)

    def step(i, carry):
        start = pl.multiple_of(i * QROWS, QROWS)
        here = pl.ds(start, QROWS)
        q = asks[pl.ds(2 * i, 2), 0:CHUNK, :].reshape(QROWS, CHUNK)
        out, gq = tile_step(q, gt[:, here], start, SELF_WIN, QROWS, True, (kx, kt, v, vt, s, e, ds, dk, dv))
        out_t[:, here] = out
        pay[pl.ds(2 * i, 2), 0:CHUNK, :] = flipped(gq.astype(BF16)).reshape(2, CHUNK, CHUNK)
        return carry

    lax.fori_loop(0, BLOCK // QROWS, step, 0, unroll=4)
    emit_sums(dk, dv, back, to_lo, to_hi)


def cross_kernel(band, vb, vl, vh, va, before, low, high, after, asks, out_t, gt, pay, back, to_lo, to_hi, kx, kt, v, vt, s, e, ds, dk, dv):
    first = band[0]
    place = lax.broadcasted_iota(jnp.int32, (16, CHUNK), 0) * CHUNK + lax.broadcasted_iota(jnp.int32, (16, CHUNK), 1)
    inside = (place >= first) & (place < first + BLOCK)
    refs = (before, low, high, after)
    bias = jnp.where(inside & (validity((vb, vl, vh, va), 1) > 0.5), 0.0, NEG)
    stage_keys(piece(refs, 0), piece(refs, CHUNK), bias, kx, kt, v, vt)
    dk[...] = jnp.zeros_like(dk)
    dv[...] = jnp.zeros_like(dv)
    start = pl.multiple_of(lax.shift_right_logical(first, 7) * CHUNK, CHUNK)

    def step(i, carry):
        here = pl.ds(pl.multiple_of(i * QROWS, QROWS), QROWS)
        q = asks[pl.ds(2 * i, 2), 2 * CHUNK : 3 * CHUNK, :].reshape(QROWS, CHUNK)
        out, gq = tile_step(q, gt[:, here], start, CROSS_WIN, 384, False, (kx, kt, v, vt, s, e, ds, dk, dv))
        both = (out + out_t[:, here]).astype(BF16)
        pay[pl.ds(2 * i, 2), 0:CHUNK, :] = flipped(both).reshape(2, CHUNK, CHUNK)
        pay[pl.ds(2 * i, 2), CHUNK : 2 * CHUNK, :] = flipped(gq.astype(BF16)).reshape(2, CHUNK, CHUNK)
        return carry

    lax.fori_loop(0, BLOCK // QROWS, step, 0, unroll=4)
    emit_sums(dk, dv, back, to_lo, to_hi)


def scratch(width):
    return [
        pltpu.VMEM((EXT, 2 * CHUNK), BF16),
        pltpu.VMEM((CHUNK, EXT), BF16),
        pltpu.VMEM((EXT, CHUNK), BF16),
        pltpu.VMEM((CHUNK, EXT), BF16),
        pltpu.VMEM((2, width, QROWS), F32),
        pltpu.VMEM((width, 2 * QROWS), BF16),
        pltpu.VMEM((width, 2 * QROWS), BF16),
        pltpu.VMEM((EXT, CHUNK), F32),
        pltpu.VMEM((EXT, CHUNK), F32),
    ]


def shaped(shape, dtype=BF16):
    return jax.ShapeDtypeStruct(shape, dtype)


def run_attention(kernel, name, width, operands, outs):
    vmem = pl.BlockSpec(memory_space=pltpu.VMEM)
    outs = outs + (shaped((8, 2 * CHUNK, CHUNK)), shaped((4, 2 * CHUNK, CHUNK)), shaped((4, 2 * CHUNK, CHUNK)))
    return pl.pallas_call(
        kernel,
        out_shape=outs,
        in_specs=[pl.BlockSpec(memory_space=pltpu.SMEM) if x.ndim == 1 else vmem for x in operands],
        out_specs=[vmem] * len(outs),
        scratch_shapes=scratch(width),
        compiler_params=pltpu.CompilerParams(vmem_limit_bytes=14 * 2**20),
        cost_estimate=pl.CostEstimate(flops=8 * 10**9, bytes_accessed=3 * 2**20, transcendentals=2621440),
        name=name,
    )(*operands)


def run_self(*operands):
    outs = (shaped((CHUNK, BLOCK), F32), shaped((CHUNK, BLOCK)), shaped((8, CHUNK, CHUNK)))
    return run_attention(self_kernel, "self_attention", SELF_WIN, operands, outs)


def run_cross(*operands):
    outs = (shaped((8, 2 * CHUNK, CHUNK)),)
    return run_attention(cross_kernel, "cross_attention", CROSS_WIN, operands, outs)


def small_call(kernel, name, pos, operands, outs):
    vmem = pl.BlockSpec(memory_space=pltpu.VMEM)
    return pl.pallas_call(
        kernel,
        out_shape=outs,
        in_specs=[pl.BlockSpec(memory_space=pltpu.SMEM)] + [vmem] * len(operands),
        out_specs=[vmem] * len(outs),
        compiler_params=pltpu.CompilerParams(vmem_limit_bytes=8 * 2**20),
        cost_estimate=pl.CostEstimate(flops=0, bytes_accessed=2**21, transcendentals=0),
        name=name,
    )(pos, *operands)


def column_pieces(pos, ref, keep, send, spot):
    for out, z in ((keep, pos[1]), (send, 1 - pos[1])):
        for d in range(4):
            first = pl.multiple_of((2 * lax.rem(pos[0] + d, 4) + z) * CHUNK, CHUNK)
            out[d, spot, :] = ref[0, :, pl.ds(first, CHUNK)]


def pack_kernel(pos, *refs):
    for n, ref in enumerate(refs[:-2]):
        column_pieces(pos, ref, *refs[-2:], slice(n * CHUNK, (n + 1) * CHUNK))


def pack(pos, *rows):
    return small_call(pack_kernel, "pack", pos, rows, (shaped((4, len(rows) * CHUNK, CHUNK)),) * 2)


def pack_marked_kernel(pos, key_valid, keys, values, keep, send, held_k, held_v, sems):
    copies = [pltpu.make_async_copy(keys, held_k, sems.at[0]), pltpu.make_async_copy(values, held_v, sems.at[1])]
    for copy in copies:
        copy.start()
    valid = key_valid[...].astype(F32)
    own = jnp.where(pos[2] == 0, valid[0:1], valid[1:2])
    other = jnp.where(pos[2] == 0, valid[1:2], valid[0:1])
    marks = jnp.concatenate([own, other, jnp.zeros((VROWS - 2, CHUNK), F32)], axis=0).astype(BF16)
    for out in (keep, send):
        for d in range(4):
            out[d, 0:VROWS, :] = marks
    for n, (copy, held) in enumerate(zip(copies, (held_k, held_v))):
        copy.wait()
        column_pieces(pos, held, keep, send, slice(VROWS + n * CHUNK, VROWS + (n + 1) * CHUNK))


def pack_marked(pos, key_valid, keys, values):
    vmem = pl.BlockSpec(memory_space=pltpu.VMEM)
    whole_hbm = pl.BlockSpec(memory_space=pl.ANY)
    return pl.pallas_call(
        pack_marked_kernel,
        out_shape=(shaped((4, VROWS + 2 * CHUNK, CHUNK)),) * 2,
        in_specs=[pl.BlockSpec(memory_space=pltpu.SMEM), vmem, whole_hbm, whole_hbm],
        out_specs=[vmem] * 2,
        scratch_shapes=[pltpu.VMEM(keys.shape, BF16), pltpu.VMEM(values.shape, BF16), pltpu.SemaphoreType.DMA((2,))],
        cost_estimate=pl.CostEstimate(flops=0, bytes_accessed=2**21, transcendentals=0),
        name="pack_marked",
    )(pos, key_valid, keys, values)


def join_kernel(pos, *refs):
    outs = refs[-4:]
    at = 0
    for keep, got in zip(refs[0:-4:2], refs[1:-4:2]):
        rows = slice(at, at + keep.shape[1])
        at += keep.shape[1]
        for d in range(4):
            outs[d][pl.ds(pos[1], 1), rows, :] = keep[d][None]
            outs[d][pl.ds(1 - pos[1], 1), rows, :] = got[d][None]


def join(pos, *pairs):
    height = sum(x.shape[1] for x in pairs[::2])
    return small_call(join_kernel, "join", pos, pairs, (shaped((2, height, CHUNK)),) * 4)


def halves_kernel(pos, *refs):
    parts, (low, high) = refs[:-2], refs[-2:]
    for d in range(4):
        y = lax.rem(pos[0] - d + 4, 4)

        @pl.when(y < 2)
        def _():
            low[pl.ds(2 * y, 2)] = parts[d][...]

        @pl.when(y >= 2)
        def _():
            high[pl.ds(2 * y - 4, 2)] = parts[d][...]


def halves(pos, parts):
    return small_call(halves_kernel, "halves", pos, parts, (shaped((4,) + parts[0].shape[1:]),) * 2)


def pack_y_kernel(pos, *refs):
    rows, outs = refs[:-4], refs[-4:]
    for n, ref in enumerate(rows):
        for d in range(4):
            first = pl.multiple_of(2 * lax.rem(pos[0] + d, 4) * CHUNK, 2 * CHUNK)
            pair = ref[0, :, pl.ds(first, 2 * CHUNK)]
            outs[d][0, n * CHUNK : (n + 1) * CHUNK, :] = pair[:, 0:CHUNK]
            outs[d][1, n * CHUNK : (n + 1) * CHUNK, :] = pair[:, CHUNK:]


def pack_y(pos, *rows):
    return small_call(pack_y_kernel, "pack_y", pos, rows, (shaped((2, len(rows) * CHUNK, CHUNK)),) * 4)


def split_kernel(pos, *refs):
    keep, send = refs[4:]
    for d in range(4):
        keep[d] = refs[d][pl.ds(pos[1], 1)][0]
        send[d] = refs[d][pl.ds(1 - pos[1], 1)][0]


def split(pos, parts):
    return small_call(split_kernel, "split", pos, parts, (shaped((4,) + parts[0].shape[1:]),) * 2)


def whole_kernel(pos, keep, got, out):
    for d in range(4):
        at = 2 * lax.rem(pos[0] - d + 4, 4)
        out[pl.ds(at + pos[1], 1)] = keep[d][None]
        out[pl.ds(at + 1 - pos[1], 1)] = got[d][None]


def whole(pos, keep, got):
    return small_call(whole_kernel, "whole", pos, (keep, got), (shaped((8,) + keep.shape[1:]),))[0]


def unpack_kernel(pos, got, *outs):
    for n, out in enumerate(outs):
        for s in range(8):
            out[0, :, s * CHUNK : (s + 1) * CHUNK] = got[s, n * CHUNK : (n + 1) * CHUNK, :]


def unpack(pos, got):
    outs = (shaped((1, CHUNK, HEADS * HEAD)),) * (got.shape[1] // CHUNK)
    return small_call(unpack_kernel, "unpack", pos, (got,), outs)


def merge_kernel(pos, *refs):
    out = refs[-1]
    for n in range(2):
        rows = slice(2 * n * CHUNK, 2 * (n + 1) * CHUNK)
        center, below, above = refs[3 * n : 3 * n + 3]
        for first, halo in ((0, below), (4, above)):
            total = center[first : first + 4].astype(F32) + halo[...].astype(F32)
            out[first : first + 4, rows, :] = total.astype(BF16)


def merge(pos, *parts):
    return small_call(merge_kernel, "merge", pos, parts, (shaped((8, 4 * CHUNK, CHUNK)),))[0]


def order_kernel(pos, *refs):
    outs = refs[-2:]
    at = 0
    for ref in refs[:-2]:
        rows = slice(at, at + ref.shape[1])
        at += ref.shape[1]
        for out, z in zip(outs, (pos[1], 1 - pos[1])):
            for d in range(4):
                out[d, rows, :] = ref[pl.ds(2 * lax.rem(pos[0] + d, 4) + z, 1)][0]


def order(pos, *parts):
    height = sum(x.shape[1] for x in parts)
    return small_call(order_kernel, "order", pos, parts, (shaped((4, height, CHUNK)),) * 2)


def unpack_parts_kernel(pos, *refs):
    parts, outs = refs[:4], refs[4:]
    for d in range(4):
        y = lax.rem(pos[0] - d + 4, 4)
        for n, out in enumerate(outs):
            for z in range(2):
                at = pl.multiple_of((2 * y + z) * CHUNK, CHUNK)
                out[0, :, pl.ds(at, CHUNK)] = parts[d][z, n * CHUNK : (n + 1) * CHUNK, :]


def unpack_parts(pos, parts):
    outs = (shaped((1, CHUNK, HEADS * HEAD)),) * (parts[0].shape[1] // CHUNK)
    return small_call(unpack_parts_kernel, "unpack_parts", pos, parts, outs)


def across_z(send):
    size = lax.axis_size("seq")
    return lax.ppermute(send, "seq", [(i, i ^ 1) for i in range(size)])


def along_y(parts):
    size = lax.axis_size("seq")
    return (parts[0],) + tuple(
        lax.ppermute(parts[d], "seq", [(i, (i + 2 * d) % size) for i in range(size)]) for d in range(1, 4)
    )


def exchange(packed):
    return lax.all_to_all(packed, "seq", split_axis=0, concat_axis=0, tiled=True)


def shards(queries, key_rows, value_rows, cross_queries, cross_keys, cross_values, grad_out, offsets, key_valid):
    tower_id = lax.axis_index("tower")
    block_id = lax.axis_index("blk")
    blocks = lax.axis_size("blk")
    up = [(b, b + 1) for b in range(blocks - 1)]
    down = [(b + 1, b) for b in range(blocks - 1)]
    over_up = [(t * blocks + b, (1 - t) * blocks + b + 1) for t in range(2) for b in range(blocks - 1)]
    over_down = [(t * blocks + b + 1, (1 - t) * blocks + b) for t in range(2) for b in range(blocks - 1)]
    swap = [(0, 1), (1, 0)]
    both = ("tower", "blk")

    seq_id = lax.axis_index("seq")
    pos = jnp.stack([seq_id // 2, seq_id % 2, tower_id]).astype(jnp.int32)
    band = (HALF + offsets[tower_id, block_id]).reshape(1)
    hold = lax.optimization_barrier
    swapped_k = lax.ppermute(cross_keys, "tower", swap)
    swapped_v = lax.ppermute(cross_values, "tower", swap)
    keep_a, send_a = pack_marked(pos, key_valid, key_rows, value_rows)
    got_a = across_z(send_a)
    keep_c, send_c = pack(pos, swapped_k, swapped_v)
    got_c = across_z(send_c)
    keep_b, send_b = split(pos, along_y(pack_y(pos, queries, grad_out, cross_queries)))
    got_b = across_z(send_b)
    low, high = halves(pos, along_y(join(pos, keep_a, got_a)))
    before = lax.ppermute(high, "blk", up)
    after = lax.ppermute(low, "blk", down)
    c_low, c_high = halves(pos, along_y(join(pos, keep_c, got_c)))
    got_b, c_low, c_high = hold((got_b, c_low, c_high))
    c_before = lax.ppermute(c_high, "blk", up)
    c_after = lax.ppermute(c_low, "blk", down)
    asks = whole(pos, keep_b, got_b)

    out_t, turned, pay_q, center, to_lo, to_hi = run_self(before, low, high, after, asks)
    above = lax.ppermute(to_lo, "blk", down)
    below = lax.ppermute(to_hi, "blk", up)
    pay_x, back, c_lo, c_hi = run_cross(
        band, before, low, high, after, c_before, c_low, c_high, c_after, asks, out_t, turned
    )
    keep_p, send_p = order(pos, pay_q, pay_x)
    got_p = across_z(send_p)
    c_above = lax.ppermute(c_lo, both, over_down)
    c_below = lax.ppermute(c_hi, both, over_up)
    c_mid = lax.ppermute(back, "tower", swap)
    got_p, center = hold((got_p, center))
    got_s = exchange(merge(pos, center, below, above, c_mid, c_below, c_above))
    g_q, attended, g_cq = unpack_parts(pos, along_y(join(pos, keep_p, got_p)))
    g_k, g_v, g_ck, g_cv = unpack(pos, got_s)
    return attended, g_q, g_k, g_v, g_cq, g_ck, g_cv


def solution(mesh):
    rows = P("tower", ("blk", "seq"), None)
    in_specs = (rows,) * 7 + (P(), P(None, ("blk", "seq")))
    return jax.shard_map(shards, mesh=mesh, in_specs=in_specs, out_specs=(rows,) * 7, check_vma=False)
```

```python
import functools

import jax
import jax.numpy as jnp
from jax import lax
from jax.experimental import pallas as pl
from jax.experimental.pallas import tpu as pltpu
from jax.sharding import PartitionSpec as P

HEADS = 16
HEAD = 64
BLOCK = 1024
HALF = 512
CHUNK = 128
QROWS = 256
EXT = BLOCK + 2 * HALF
SELF_WIN = QROWS + 2 * HALF
CROSS_WIN = BLOCK + CHUNK
NEG = -16384.0
SCALE = HEAD**-0.5
VROWS = 16
F32 = jnp.float32
BF16 = jnp.bfloat16
NT = (((1,), (1,)), ((), ()))
NN = (((1,), (0,)), ((), ()))


def dot(a, b, dims=NN):
    return lax.dot_general(a, b, dims, preferred_element_type=F32)


def eye(n):
    rows = lax.broadcasted_iota(jnp.int32, (n, n), 0)
    return jnp.where(rows == lax.broadcasted_iota(jnp.int32, (n, n), 1), 1.0, 0.0).astype(BF16)


def flipped(x):
    return dot(eye(x.shape[1]), x, NT).astype(BF16)


def stage_keys(chunks, values, bias, kx, kt, v, vt):
    padded = jnp.concatenate([bias, jnp.zeros((CHUNK - 16, CHUNK), F32)], axis=0).astype(BF16)
    turned = dot(eye(CHUNK), padded, NT)
    lane = lax.broadcasted_iota(jnp.int32, (CHUNK, CHUNK), 1)
    for c in range(0, EXT // CHUNK, 2):
        pair = pl.ds(c * CHUNK, 2 * CHUNK)
        k = jnp.concatenate([chunks(c), chunks(c + 1)], axis=0)
        val = jnp.concatenate([values(c), values(c + 1)], axis=0)
        kx[pair, 0:CHUNK] = k
        for n in range(2):
            kx[pl.ds((c + n) * CHUNK, CHUNK), CHUNK : 2 * CHUNK] = jnp.where(lane == c + n, turned, 0.0).astype(BF16)
        kt[:, pair] = flipped(k)
        v[pair, :] = val
        vt[:, pair] = flipped(val)


def tile_step(q, gt, start, width, step, windowed, scratch):
    kx, kt, v, vt, s, e, ds, dk, dv = scratch
    count = width // step
    head_lane = lax.broadcasted_iota(jnp.int32, (QROWS, 2 * HEAD), 1) // HEAD
    scaled = q.astype(F32) * SCALE
    ones = jnp.ones((QROWS, CHUNK), BF16)
    win = pl.ds(start, width)
    outs, gqs, q_heads, g_heads, tops, dots = [], [], [], [], [], []
    for h in range(2):
        qh = jnp.where(head_lane == h, scaled, 0.0).astype(BF16)
        qx = jnp.concatenate([qh, ones], axis=1)
        q_heads.append(qh)
        top = None
        for b in range(count):
            at = pl.ds(start + b * step, step)
            scores = dot(kx[at, :], qx, NT)
            if windowed and b in (0, count - 1):
                r = lax.broadcasted_iota(jnp.int32, (step, QROWS), 0)
                c = lax.broadcasted_iota(jnp.int32, (step, QROWS), 1)
                scores = jnp.where(r >= c if b == 0 else r <= c, scores, -1e30)
            s[h, b * step : (b + 1) * step, :] = scores
            high = jnp.max(scores, axis=0, keepdims=True)
            top = high if top is None else jnp.maximum(top, high)
        tops.append(top)
    for h in range(2):
        rows_h = slice(h * HEAD, (h + 1) * HEAD)
        cols_h = slice(h * QROWS, (h + 1) * QROWS)
        total = jnp.zeros((1, QROWS), F32)
        for b in range(count):
            rows = slice(b * step, (b + 1) * step)
            p = jnp.exp(s[h, rows, :] - tops[h])
            total = total + jnp.sum(p, axis=0, keepdims=True)
            e[rows, cols_h] = p.astype(BF16)
        inverse = 1.0 / total
        out = dot(vt[rows_h, win], e[:, cols_h]) * inverse
        g = (gt[rows_h, :].astype(F32) * inverse).astype(BF16)
        dots.append(jnp.sum(out * g.astype(F32), axis=0, keepdims=True))
        zeros = jnp.zeros((HEAD, QROWS), BF16)
        g_heads.append(jnp.concatenate([g, zeros] if h == 0 else [zeros, g], axis=0))
        outs.append(out)
    for h in range(2):
        rows_h = slice(h * HEAD, (h + 1) * HEAD)
        cols_h = slice(h * QROWS, (h + 1) * QROWS)
        for b in range(count):
            rows = slice(b * step, (b + 1) * step)
            at = pl.ds(start + b * step, step)
            dp = dot(v[at, :], g_heads[h])
            ds[rows, cols_h] = (e[rows, cols_h].astype(F32) * (dp - dots[h])).astype(BF16)
        gqs.append(dot(kt[rows_h, win], ds[:, cols_h]) * SCALE)
    dv[win, :] += dot(e[...], jnp.concatenate(g_heads, axis=1), NT)
    dk[win, :] += dot(ds[...], jnp.concatenate(q_heads, axis=0))
    return jnp.concatenate(outs, axis=0), jnp.concatenate(gqs, axis=0)


def validity(refs, row):
    parts = [ref[c, 0:VROWS, :].astype(F32)[row : row + 1] for ref in refs for c in range(4)]
    return jnp.concatenate(parts, axis=0)


def piece(refs, first):
    return lambda c: refs[c // 4][c % 4, first : first + CHUNK, :]


def emit_sums(dk, dv, back, to_lo, to_hi, first):
    for n, acc in enumerate((dk, dv)):
        rows = slice(n * CHUNK, (n + 1) * CHUNK)
        share = slice(first + n * CHUNK, first + (n + 1) * CHUNK)
        to_lo[:, share, :] = acc[0:HALF, :].astype(BF16).reshape(4, CHUNK, CHUNK)
        back[:, rows, :] = acc[HALF : HALF + BLOCK, :].astype(BF16).reshape(8, CHUNK, CHUNK)
        to_hi[:, share, :] = acc[HALF + BLOCK : EXT, :].astype(BF16).reshape(4, CHUNK, CHUNK)


def self_kernel(before, low, high, after, asks, out_t, gt, pay, back, to_lo, to_hi, kx, kt, v, vt, s, e, ds, dk, dv):
    refs = (before, low, high, after)
    bias = jnp.where(validity(refs, 0) > 0.5, 0.0, NEG)
    stage_keys(piece(refs, VROWS), piece(refs, VROWS + CHUNK), bias, kx, kt, v, vt)
    for c in range(0, 8, 2):
        pair = jnp.concatenate([asks[c, CHUNK : 2 * CHUNK, :], asks[c + 1, CHUNK : 2 * CHUNK, :]], axis=0)
        gt[:, c * CHUNK : (c + 2) * CHUNK] = flipped(pair)
    dk[...] = jnp.zeros_like(dk)
    dv[...] = jnp.zeros_like(dv)

    def step(i, carry):
        start = pl.multiple_of(i * QROWS, QROWS)
        here = pl.ds(start, QROWS)
        q = asks[pl.ds(2 * i, 2), 0:CHUNK, :].reshape(QROWS, CHUNK)
        out, gq = tile_step(q, gt[:, here], start, SELF_WIN, QROWS, True, (kx, kt, v, vt, s, e, ds, dk, dv))
        out_t[:, here] = out
        pay[pl.ds(2 * i, 2), 0:CHUNK, :] = flipped(gq.astype(BF16)).reshape(2, CHUNK, CHUNK)
        return carry

    lax.fori_loop(0, BLOCK // QROWS, step, 0, unroll=4)
    emit_sums(dk, dv, back, to_lo, to_hi, 0)


def cross_kernel(band, vb, vl, vh, va, before, low, high, after, asks, out_t, gt, self_lo, self_hi, pay, back, to_lo, to_hi, kx, kt, v, vt, s, e, ds, dk, dv):
    to_lo[:, 0 : 2 * CHUNK, :] = self_lo[...]
    to_hi[:, 0 : 2 * CHUNK, :] = self_hi[...]
    first = band[0]
    place = lax.broadcasted_iota(jnp.int32, (16, CHUNK), 0) * CHUNK + lax.broadcasted_iota(jnp.int32, (16, CHUNK), 1)
    inside = (place >= first) & (place < first + BLOCK)
    refs = (before, low, high, after)
    bias = jnp.where(inside & (validity((vb, vl, vh, va), 1) > 0.5), 0.0, NEG)
    stage_keys(piece(refs, 0), piece(refs, CHUNK), bias, kx, kt, v, vt)
    dk[...] = jnp.zeros_like(dk)
    dv[...] = jnp.zeros_like(dv)
    start = pl.multiple_of(lax.shift_right_logical(first, 7) * CHUNK, CHUNK)

    def step(i, carry):
        here = pl.ds(pl.multiple_of(i * QROWS, QROWS), QROWS)
        q = asks[pl.ds(2 * i, 2), 2 * CHUNK : 3 * CHUNK, :].reshape(QROWS, CHUNK)
        out, gq = tile_step(q, gt[:, here], start, CROSS_WIN, 384, False, (kx, kt, v, vt, s, e, ds, dk, dv))
        both = (out + out_t[:, here]).astype(BF16)
        pay[pl.ds(2 * i, 2), 0:CHUNK, :] = flipped(both).reshape(2, CHUNK, CHUNK)
        pay[pl.ds(2 * i, 2), CHUNK : 2 * CHUNK, :] = flipped(gq.astype(BF16)).reshape(2, CHUNK, CHUNK)
        return carry

    lax.fori_loop(0, BLOCK // QROWS, step, 0, unroll=4)
    emit_sums(dk, dv, back, to_lo, to_hi, 2 * CHUNK)


def scratch(width):
    return [
        pltpu.VMEM((EXT, 2 * CHUNK), BF16),
        pltpu.VMEM((CHUNK, EXT), BF16),
        pltpu.VMEM((EXT, CHUNK), BF16),
        pltpu.VMEM((CHUNK, EXT), BF16),
        pltpu.VMEM((2, width, QROWS), F32),
        pltpu.VMEM((width, 2 * QROWS), BF16),
        pltpu.VMEM((width, 2 * QROWS), BF16),
        pltpu.VMEM((EXT, CHUNK), F32),
        pltpu.VMEM((EXT, CHUNK), F32),
    ]


def shaped(shape, dtype=BF16):
    return jax.ShapeDtypeStruct(shape, dtype)


def run_attention(kernel, name, width, operands, outs, share):
    vmem = pl.BlockSpec(memory_space=pltpu.VMEM)
    outs = outs + (shaped((8, 2 * CHUNK, CHUNK)), shaped((4, share, CHUNK)), shaped((4, share, CHUNK)))
    return pl.pallas_call(
        kernel,
        out_shape=outs,
        in_specs=[pl.BlockSpec(memory_space=pltpu.SMEM) if x.ndim == 1 else vmem for x in operands],
        out_specs=[vmem] * len(outs),
        scratch_shapes=scratch(width),
        compiler_params=pltpu.CompilerParams(vmem_limit_bytes=14 * 2**20),
        cost_estimate=pl.CostEstimate(flops=8 * 10**9, bytes_accessed=3 * 2**20, transcendentals=2621440),
        name=name,
    )(*operands)


def run_self(*operands):
    outs = (shaped((CHUNK, BLOCK), F32), shaped((CHUNK, BLOCK)), shaped((8, CHUNK, CHUNK)))
    return run_attention(self_kernel, "self_attention", SELF_WIN, operands, outs, 2 * CHUNK)


def run_cross(*operands):
    outs = (shaped((8, 2 * CHUNK, CHUNK)),)
    return run_attention(cross_kernel, "cross_attention", CROSS_WIN, operands, outs, 4 * CHUNK)


def small_call(kernel, name, pos, operands, outs):
    vmem = pl.BlockSpec(memory_space=pltpu.VMEM)
    return pl.pallas_call(
        kernel,
        out_shape=outs,
        in_specs=[pl.BlockSpec(memory_space=pltpu.SMEM)] + [vmem] * len(operands),
        out_specs=[vmem] * len(outs),
        compiler_params=pltpu.CompilerParams(vmem_limit_bytes=8 * 2**20),
        cost_estimate=pl.CostEstimate(flops=0, bytes_accessed=2**21, transcendentals=0),
        name=name,
    )(pos, *operands)


def column_pieces(pos, ref, keep, send, spot):
    for out, z in ((keep, pos[1]), (send, 1 - pos[1])):
        for d in range(4):
            first = pl.multiple_of((2 * lax.rem(pos[0] + d, 4) + z) * CHUNK, CHUNK)
            out[d, spot, :] = ref[0, :, pl.ds(first, CHUNK)]


def pack_kernel(pos, *refs):
    for n, ref in enumerate(refs[:-2]):
        column_pieces(pos, ref, *refs[-2:], slice(n * CHUNK, (n + 1) * CHUNK))


def pack(pos, *rows):
    return small_call(pack_kernel, "pack", pos, rows, (shaped((4, len(rows) * CHUNK, CHUNK)),) * 2)


def pack_marked_kernel(pos, key_valid, keys, values, keep, send, held_k, held_v, sems):
    copies = [pltpu.make_async_copy(keys, held_k, sems.at[0]), pltpu.make_async_copy(values, held_v, sems.at[1])]
    for copy in copies:
        copy.start()
    valid = key_valid[...].astype(F32)
    own = jnp.where(pos[2] == 0, valid[0:1], valid[1:2])
    other = jnp.where(pos[2] == 0, valid[1:2], valid[0:1])
    marks = jnp.concatenate([own, other, jnp.zeros((VROWS - 2, CHUNK), F32)], axis=0).astype(BF16)
    for out in (keep, send):
        for d in range(4):
            out[d, 0:VROWS, :] = marks
    for n, (copy, held) in enumerate(zip(copies, (held_k, held_v))):
        copy.wait()
        column_pieces(pos, held, keep, send, slice(VROWS + n * CHUNK, VROWS + (n + 1) * CHUNK))


def pack_marked(pos, key_valid, keys, values):
    vmem = pl.BlockSpec(memory_space=pltpu.VMEM)
    whole_hbm = pl.BlockSpec(memory_space=pl.ANY)
    return pl.pallas_call(
        pack_marked_kernel,
        out_shape=(shaped((4, VROWS + 2 * CHUNK, CHUNK)),) * 2,
        in_specs=[pl.BlockSpec(memory_space=pltpu.SMEM), vmem, whole_hbm, whole_hbm],
        out_specs=[vmem] * 2,
        scratch_shapes=[pltpu.VMEM(keys.shape, BF16), pltpu.VMEM(values.shape, BF16), pltpu.SemaphoreType.DMA((2,))],
        cost_estimate=pl.CostEstimate(flops=0, bytes_accessed=2**21, transcendentals=0),
        name="pack_marked",
    )(pos, key_valid, keys, values)


def join_kernel(pos, *refs):
    outs = refs[-4:]
    at = 0
    for keep, got in zip(refs[0:-4:2], refs[1:-4:2]):
        rows = slice(at, at + keep.shape[1])
        at += keep.shape[1]
        for d in range(4):
            outs[d][pl.ds(pos[1], 1), rows, :] = keep[d][None]
            outs[d][pl.ds(1 - pos[1], 1), rows, :] = got[d][None]


def join(pos, *pairs):
    height = sum(x.shape[1] for x in pairs[::2])
    return small_call(join_kernel, "join", pos, pairs, (shaped((2, height, CHUNK)),) * 4)


def halves_kernel(pos, *refs):
    parts, (low, high) = refs[:-2], refs[-2:]
    for d in range(4):
        y = lax.rem(pos[0] - d + 4, 4)

        @pl.when(y < 2)
        def _():
            low[pl.ds(2 * y, 2)] = parts[d][...]

        @pl.when(y >= 2)
        def _():
            high[pl.ds(2 * y - 4, 2)] = parts[d][...]


def halves(pos, parts):
    return small_call(halves_kernel, "halves", pos, parts, (shaped((4,) + parts[0].shape[1:]),) * 2)


def pack_y_kernel(pos, *refs):
    rows, outs = refs[:-4], refs[-4:]
    for n, ref in enumerate(rows):
        for d in range(4):
            first = pl.multiple_of(2 * lax.rem(pos[0] + d, 4) * CHUNK, 2 * CHUNK)
            pair = ref[0, :, pl.ds(first, 2 * CHUNK)]
            outs[d][0, n * CHUNK : (n + 1) * CHUNK, :] = pair[:, 0:CHUNK]
            outs[d][1, n * CHUNK : (n + 1) * CHUNK, :] = pair[:, CHUNK:]


def pack_y(pos, *rows):
    return small_call(pack_y_kernel, "pack_y", pos, rows, (shaped((2, len(rows) * CHUNK, CHUNK)),) * 4)


def split_kernel(pos, *refs):
    keep, send = refs[4:]
    for d in range(4):
        keep[d] = refs[d][pl.ds(pos[1], 1)][0]
        send[d] = refs[d][pl.ds(1 - pos[1], 1)][0]


def split(pos, parts):
    return small_call(split_kernel, "split", pos, parts, (shaped((4,) + parts[0].shape[1:]),) * 2)


def whole_kernel(pos, keep, got, out):
    for d in range(4):
        at = 2 * lax.rem(pos[0] - d + 4, 4)
        out[pl.ds(at + pos[1], 1)] = keep[d][None]
        out[pl.ds(at + 1 - pos[1], 1)] = got[d][None]


def whole(pos, keep, got):
    return small_call(whole_kernel, "whole", pos, (keep, got), (shaped((8,) + keep.shape[1:]),))[0]


def unpack_kernel(pos, got, *outs):
    for n, out in enumerate(outs):
        for s in range(8):
            out[0, :, s * CHUNK : (s + 1) * CHUNK] = got[s, n * CHUNK : (n + 1) * CHUNK, :]


def unpack(pos, got):
    outs = (shaped((1, CHUNK, HEADS * HEAD)),) * (got.shape[1] // CHUNK)
    return small_call(unpack_kernel, "unpack", pos, (got,), outs)


def merge_kernel(pos, *refs):
    out = refs[-1]
    for n in range(2):
        rows = slice(2 * n * CHUNK, 2 * (n + 1) * CHUNK)
        center, below, above = refs[3 * n : 3 * n + 3]
        for first, halo in ((0, below), (4, above)):
            total = center[first : first + 4].astype(F32) + halo[:, 0 : 2 * CHUNK, :].astype(F32)
            out[first : first + 4, rows, :] = total.astype(BF16)


def merge(pos, *parts):
    return small_call(merge_kernel, "merge", pos, parts, (shaped((8, 4 * CHUNK, CHUNK)),))[0]


def order_kernel(pos, *refs):
    outs = refs[-2:]
    at = 0
    for ref in refs[:-2]:
        rows = slice(at, at + ref.shape[1])
        at += ref.shape[1]
        for out, z in zip(outs, (pos[1], 1 - pos[1])):
            for d in range(4):
                out[d, rows, :] = ref[pl.ds(2 * lax.rem(pos[0] + d, 4) + z, 1)][0]


def order(pos, *parts):
    height = sum(x.shape[1] for x in parts)
    return small_call(order_kernel, "order", pos, parts, (shaped((4, height, CHUNK)),) * 2)


def unpack_parts_kernel(pos, *refs):
    parts, outs = refs[:4], refs[4:]
    for d in range(4):
        y = lax.rem(pos[0] - d + 4, 4)
        for n, out in enumerate(outs):
            for z in range(2):
                at = pl.multiple_of((2 * y + z) * CHUNK, CHUNK)
                out[0, :, pl.ds(at, CHUNK)] = parts[d][z, n * CHUNK : (n + 1) * CHUNK, :]


def unpack_parts(pos, parts):
    outs = (shaped((1, CHUNK, HEADS * HEAD)),) * (parts[0].shape[1] // CHUNK)
    return small_call(unpack_parts_kernel, "unpack_parts", pos, parts, outs)


def across_z(send):
    size = lax.axis_size("seq")
    return lax.ppermute(send, "seq", [(i, i ^ 1) for i in range(size)])


def along_y(parts):
    size = lax.axis_size("seq")
    return (parts[0],) + tuple(
        lax.ppermute(parts[d], "seq", [(i, (i + 2 * d) % size) for i in range(size)]) for d in range(1, 4)
    )


def exchange(packed):
    return lax.all_to_all(packed, "seq", split_axis=0, concat_axis=0, tiled=True)


def shards(queries, key_rows, value_rows, cross_queries, cross_keys, cross_values, grad_out, offsets, key_valid):
    tower_id = lax.axis_index("tower")
    block_id = lax.axis_index("blk")
    blocks = lax.axis_size("blk")
    up = [(b, b + 1) for b in range(blocks - 1)]
    down = [(b + 1, b) for b in range(blocks - 1)]
    over_up = [(t * blocks + b, (1 - t) * blocks + b + 1) for t in range(2) for b in range(blocks - 1)]
    over_down = [(t * blocks + b + 1, (1 - t) * blocks + b) for t in range(2) for b in range(blocks - 1)]
    swap = [(0, 1), (1, 0)]
    both = ("tower", "blk")

    seq_id = lax.axis_index("seq")
    pos = jnp.stack([seq_id // 2, seq_id % 2, tower_id]).astype(jnp.int32)
    band = (HALF + offsets[tower_id, block_id]).reshape(1)
    hold = lax.optimization_barrier
    swapped_k = lax.ppermute(cross_keys, "tower", swap)
    swapped_v = lax.ppermute(cross_values, "tower", swap)
    keep_a, send_a = pack_marked(pos, key_valid, key_rows, value_rows)
    got_a = across_z(send_a)
    keep_c, send_c = pack(pos, swapped_k, swapped_v)
    got_c = across_z(send_c)
    keep_b, send_b = split(pos, along_y(pack_y(pos, queries, grad_out, cross_queries)))
    got_b = across_z(send_b)
    low, high = halves(pos, along_y(join(pos, keep_a, got_a)))
    before = lax.ppermute(high, "blk", up)
    after = lax.ppermute(low, "blk", down)
    c_low, c_high = halves(pos, along_y(join(pos, keep_c, got_c)))
    got_b, c_low, c_high = hold((got_b, c_low, c_high))
    c_before = lax.ppermute(c_high, "blk", up)
    c_after = lax.ppermute(c_low, "blk", down)
    asks = whole(pos, keep_b, got_b)

    out_t, turned, pay_q, center, to_lo, to_hi = run_self(before, low, high, after, asks)
    pay_x, back, c_lo, c_hi = run_cross(
        band, before, low, high, after, c_before, c_low, c_high, c_after, asks, out_t, turned, to_lo, to_hi
    )
    keep_p, send_p = order(pos, pay_q, pay_x)
    got_p = across_z(send_p)
    above = lax.ppermute(c_lo, "blk", down)
    below = lax.ppermute(c_hi, "blk", up)
    c_above = lax.ppermute(above[:, 2 * CHUNK :], "tower", swap)
    c_below = lax.ppermute(below[:, 2 * CHUNK :], "tower", swap)
    c_mid = lax.ppermute(back, "tower", swap)
    got_p, center = hold((got_p, center))
    got_s = exchange(merge(pos, center, below, above, c_mid, c_below, c_above))
    g_q, attended, g_cq = unpack_parts(pos, along_y(join(pos, keep_p, got_p)))
    g_k, g_v, g_ck, g_cv = unpack(pos, got_s)
    return attended, g_q, g_k, g_v, g_cq, g_ck, g_cv


def solution(mesh):
    rows = P("tower", ("blk", "seq"), None)
    in_specs = (rows,) * 7 + (P(), P(None, ("blk", "seq")))
    return jax.shard_map(shards, mesh=mesh, in_specs=in_specs, out_specs=(rows,) * 7, check_vma=False)
```
